32 devices in a mesh: node: 8 (over y, x, core), centre: 4 (over z).
Axes of the slice: x: 2, y: 2, z: 4, core: 2. Of those that a mesh axis runs over, the one named last changes fastest.
Arguments:
- node_coords: float32 [3, 32768], P(None, ('node', 'centre')), may hold values from 0 to 1
- centre_coords: float32 [3, 16384], P(None, ('centre', 'node')), may hold values from 0 to 1
- disp_coef: float32 [6, 16384], P(None, ('centre', 'node')), may hold values from -3 to 3
- send_count: int32 [8, 8], P('node'), may hold values from 1 to 1024, 4096 in all within a row
- send_order: int32 [8, 4096], P('node'), may hold values from 0 to 4095, each once within a row
- slot_perm: int32 [8, 8192], P('node'), may hold values from 0 to 8191, each once within a row
- fluid_force: float32 [3, 65536], P(None, 'node'), may hold values from -2 to 2
Outputs:
- fluid_disp: float32 [6, 65536], P(None, 'node')
- centre_force: float32 [3, 16384], P(None, ('centre', 'node'))
The draws below stay inside these ranges and needn't reach their ends.
Inputs may be any that keep to these rules, and one draw needn't show every extreme that they name: `send_count`: each row sums to 4096; each row's largest entry is 1024. `send_order`: each row is a permutation. `slot_perm`: each row is a permutation.
All inputs are finite; a program needn't handle non-finite values.
Results may differ from the reference program's by a relative error of at most 0.0003.
Values sent between devices are 32-bit elements; how exact they have to be, the bound alone decides.
A program may use at most 64 MiB of HBM per device.

```python
import math
import jax
import jax.numpy as jnp
import numpy as np
from jax import lax

NODE_DEV = 4096
SUPPORT = 192
NODES = 32768
CENTRES = 16384
CAP = 1024
FLUID_DEV = 8192
FLUID = 65536
N_NODE = 8


def steps_of(own_key, dims, cuts, smallest, high):
    factor_of, own = 1.0, jax.random.fold_in(own_key, 6)
    for dim, blocks in cuts:
        heights = jnp.exp(jax.random.uniform(jax.random.fold_in(own, dim), (blocks,), jnp.float32, smallest / len(cuts), high / len(cuts)))
        factor_of = factor_of * jnp.repeat(heights, dims[dim] // blocks).reshape([-1 if axis == dim else 1 for axis in range(len(dims))])
    return factor_of


def length_profile(number_of, total, reach, skew):
    portions = [(1 << 20) // math.isqrt(rank ** skew) + 1 for rank in range(2, number_of + 1)]
    spare, counts = total - reach - (number_of - 1), [1] * (number_of - 1)
    while spare > 0:
        movable = [i for i in range(number_of - 1) if counts[i] < reach]
        mass, budget = sum([portions[i] for i in movable]), spare
        for i in movable:
            extra = min(reach - counts[i], max(1, budget * portions[i] // mass), spare)
            counts[i] = counts[i] + extra
            spare = spare - extra
    return np.array([reach] + counts)


def ragged(rng, amount, total, reach, skew):
    if amount == 2:
        one = jax.random.randint(rng, (), max(1, total - reach), min(reach, total - 1) + 1)
        return jnp.stack([one, total - one])
    sizes = jnp.asarray(length_profile(amount, total, reach, skew), jnp.int32)
    couples = (amount - 1) // 2
    source_of, taker = sizes[1:1 + 2 * couples:2], sizes[2:2 + 2 * couples:2]
    room = jnp.minimum(source_of - 1, reach - taker)
    shifted = jax.random.randint(jax.random.fold_in(rng, 1), (couples,), 0, 1 << 20) % (room + 1)
    sizes = sizes.at[1:1 + 2 * couples:2].set(source_of - shifted).at[2:2 + 2 * couples:2].set(taker + shifted)
    return sizes[jax.random.permutation(jax.random.fold_in(rng, 2), amount)]


def bell_draw(rng, extent, spread, reach, shards=(), held_as=jnp.bfloat16):
    drawn = jax.random.normal(rng, extent, jnp.float32) * spread
    if len(shards) > 0:
        drawn = steps_of(rng, extent, shards, -0.22, 0.18) * drawn
    return jnp.clip(drawn, min=-reach, max=reach).astype(held_as)


def setup_inputs(seed: int = 0) -> dict:
    splits = jax.random.split(jax.random.key(seed), 8)
    node_coords = jnp.clip(1.0 * jax.random.uniform(splits[0], (3, NODES), jnp.float32) ** steps_of(splits[0], (3, NODES), ((1, 32),), -0.2, 0.2), 0.0, 1.0)
    centre_coords = jnp.clip(1.0 * jax.random.uniform(splits[1], (3, CENTRES), jnp.float32) ** steps_of(splits[1], (3, CENTRES), ((1, 32),), -0.2, 0.2), 0.0, 1.0)
    disp_coef = bell_draw(splits[2], (6, CENTRES), (max(SUPPORT // 40, 1)) ** -0.5, 3.0, ((1, 32),), jnp.float32)
    send_count = jax.vmap(lambda own: ragged(own, N_NODE, NODE_DEV, CAP, 2))(jax.random.split(splits[3], N_NODE)).reshape((N_NODE, N_NODE)).astype(jnp.int32)
    send_order = jax.vmap(lambda own: jax.random.permutation(own, NODE_DEV))(jax.random.split(splits[4], N_NODE)).reshape((N_NODE, NODE_DEV)).astype(jnp.int32)
    slot_perm = jax.vmap(lambda own: jax.random.permutation(own, FLUID_DEV))(jax.random.split(splits[5], N_NODE)).reshape((N_NODE, FLUID_DEV)).astype(jnp.int32)
    fluid_force = bell_draw(splits[6], (3, FLUID), (max(SUPPORT * NODES // (40 * CENTRES), 1)) ** -0.5, 2.0, ((1, 8),), jnp.float32)
    return {"node_coords": node_coords, "centre_coords": centre_coords, "disp_coef": disp_coef, "send_count": send_count, "send_order": send_order, "slot_perm": slot_perm, "fluid_force": fluid_force}


def kernel(points, centres, radius):
    squared = (points[0][:, None] - centres[0][None, :]) ** 2
    squared = squared + (points[1][:, None] - centres[1][None, :]) ** 2
    squared = squared + (points[2][:, None] - centres[2][None, :]) ** 2
    scaled = jnp.sqrt(squared) / radius
    remain = jnp.maximum(1.0 - scaled, 0.0)
    return remain ** 4 * (4.0 * scaled + 1.0)

def pick_row(order_row, places):
    return order_row[places]

def reorder_row(received, order_row):
    return received[:, order_row]

def reference(node_coords, centre_coords, disp_coef, send_count, send_order, slot_perm, fluid_force):
    radius = (0.75 * SUPPORT / (math.pi * CENTRES)) ** (1.0 / 3.0)
    offsets = jnp.cumsum(send_count, axis=1) - send_count
    slot_ids = jnp.arange(CAP, dtype=jnp.int32)
    filled = slot_ids[None, None, :] < send_count[:, :, None]
    places = jnp.minimum(offsets[:, :, None] + slot_ids[None, None, :], NODE_DEV - 1).astype(jnp.int32)
    picked = jax.vmap(pick_row)(send_order, places)
    global_ids = picked + (jnp.arange(N_NODE, dtype=jnp.int32) * NODE_DEV)[:, None, None]
    inverse = jnp.argsort(slot_perm, axis=1).astype(jnp.int32)
    positions = inverse.reshape(N_NODE, N_NODE, CAP) + (jnp.arange(N_NODE, dtype=jnp.int32) * FLUID_DEV)[:, None, None]
    returned = jnp.transpose(fluid_force[:, positions], (0, 2, 1, 3))
    returned = jnp.where(filled[None], returned, 0.0)
    wall_force = jnp.zeros((3, NODES), jnp.float32).at[:, global_ids.reshape(-1)].add(returned.reshape(3, -1))
    block_rows = math.gcd(NODES, 1024)
    point_blocks = jnp.transpose(node_coords.reshape(3, NODES // block_rows, block_rows), (1, 0, 2))
    force_blocks = jnp.transpose(wall_force.reshape(3, NODES // block_rows, block_rows), (1, 0, 2))

    def advance(running, pieces):
        block_pts, forces = pieces
        basis = kernel(block_pts, centre_coords, radius)
        disp = lax.dot_general(disp_coef, basis, (((1,), (1,)), ((), ())), precision=lax.Precision.HIGHEST, preferred_element_type=jnp.float32)
        running = running + jnp.dot(forces, basis, precision=lax.Precision.HIGHEST, preferred_element_type=jnp.float32)
        return (running, disp)
    centre_force, disp_blocks = lax.scan(advance, jnp.zeros((3, CENTRES), jnp.float32), (point_blocks, force_blocks))
    wall_disp = jnp.transpose(disp_blocks, (1, 0, 2)).reshape(6, NODES)
    sent_disp = jnp.where(filled[None], wall_disp[:, global_ids], 0.0)
    by_owner = jnp.transpose(sent_disp, (2, 0, 1, 3)).reshape(N_NODE, 6, FLUID_DEV)
    fluid_rows = jax.vmap(reorder_row)(by_owner, slot_perm)
    fluid_disp = jnp.transpose(fluid_rows, (1, 0, 2)).reshape(6, FLUID)
    return (fluid_disp, centre_force)
```

```python
import functools
import math

import jax
import jax.numpy as jnp
from jax import lax
from jax.experimental import pallas as pl
from jax.experimental.pallas import tpu as pltpu
from jax.sharding import PartitionSpec as P

SUPPORT = 192
LANES = 128
F32 = jnp.float32
BF16 = jnp.bfloat16
VMEM_BYTES = 48 * 1024 * 1024
NT = (((1,), (1,)), ((), ()))


def vmem():
    return pl.BlockSpec(memory_space=pltpu.VMEM)


def smem():
    return pl.BlockSpec(memory_space=pltpu.SMEM)


def split(value):
    high = value.astype(BF16).astype(F32)
    return high, value - high


def onehot(index, rows):
    lanes = index.shape[1]
    return jnp.where(lax.broadcasted_iota(jnp.int32, (rows, lanes), 0) == index, 1.0, 0.0)


def scatter_part(values, index, high_rows):
    n = index.shape[1]
    low = jnp.bitwise_and(index, LANES - 1)
    high = lax.shift_right_arithmetic(index, 7)
    low_hot = onehot(low, LANES).astype(BF16)
    mask = lax.broadcasted_iota(jnp.int32, (high_rows, n), 0) == high
    stacked = jnp.concatenate(
        [jnp.where(mask, value, 0.0).astype(BF16) for value in values], axis=0
    )
    return lax.dot_general(stacked, low_hot, NT, preferred_element_type=F32)


def gather_part(lhs, index, high_rows, channels):
    n = index.shape[1]
    low = jnp.bitwise_and(index, LANES - 1)
    high = lax.shift_right_arithmetic(index, 7)
    hot = onehot(high, high_rows).astype(BF16)
    hot = jnp.concatenate([hot, hot], axis=0)
    wide = jnp.dot(lhs, hot, preferred_element_type=F32)
    mask = lax.broadcasted_iota(jnp.int32, (LANES, n), 0) == low
    rows = [
        jnp.sum(
            jnp.where(mask, wide[c * LANES : (c + 1) * LANES], 0.0), axis=0, keepdims=True
        )
        for c in range(channels)
    ]
    return jnp.concatenate(rows, axis=0)


def prepare_kernel(n_node, rows, count_ref, order_ref, perm_ref, force_ref, send_ref, index_ref, acc_ref):
    fluid_dev = perm_ref.shape[1]
    high_rows = fluid_dev // LANES
    node_rows = order_ref.shape[0]
    capacity = rows * LANES
    step = 1024
    for start in range(0, fluid_dev, step):
        values = []
        for c in range(3):
            values.extend(split(force_ref[c : c + 1, start : start + step]))
        part = scatter_part(values, perm_ref[:, start : start + step], high_rows)
        if start == 0:
            acc_ref[...] = part
        else:
            acc_ref[...] += part
    for c in range(3):
        base = 2 * c * high_rows
        for b in range(n_node):
            lo = base + b * rows
            send_ref[b, c * rows : (c + 1) * rows, :] = (
                acc_ref[lo : lo + rows, :]
                + acc_ref[lo + high_rows : lo + high_rows + rows, :]
            )
    high, low = split(order_ref[...].astype(F32))
    lhs = jnp.transpose(
        jnp.concatenate([high, low, jnp.zeros((LANES - 2 * node_rows, LANES), F32)], axis=0)
    ).astype(BF16)[:, : 2 * node_rows]
    offset = jnp.int32(0)
    for o in range(n_node):
        count = count_ref[0, o]
        slot = lax.broadcasted_iota(jnp.int32, (1, capacity), 1)
        place = jnp.minimum(offset + slot, node_rows * LANES - 1)
        found = gather_part(lhs, place, node_rows, 1).astype(jnp.int32)
        found = jnp.where(slot < count, found, -1)
        index_ref[:, o * capacity : (o + 1) * capacity] = found
        offset = offset + count


def greet(axes):
    barrier = pltpu.get_barrier_semaphore()
    total = 0
    for name, size in axes:
        me = lax.axis_index(name)
        for d in range(1, size):
            pl.semaphore_signal(
                barrier, inc=1, device_id={name: lax.rem(me + d, size)},
                device_id_type=pl.DeviceIdType.MESH,
            )
            total += 1
    pl.semaphore_wait(barrier, total)


def spread(name, size, source, target, send_sem, recv_sem, gather):
    me = lax.axis_index(name)
    copies = []
    for d in range(1, size):
        peer = lax.rem(me + d, size)
        copy = pltpu.make_async_remote_copy(
            src_ref=source if gather else source.at[peer],
            dst_ref=target.at[me],
            send_sem=send_sem.at[d],
            recv_sem=recv_sem.at[d],
            device_id={name: peer},
            device_id_type=pl.DeviceIdType.MESH,
        )
        copy.start()
        copies.append(copy)
    return copies


def gather_kernel(
    n_node, n_centre, node_ref, centre_ref, coef_ref, send_ref,
    points_ref, centres_ref, coeffs_ref, recv_ref, sem_a, sem_b, sem_c, sem_d,
):
    greet((("node", n_node), ("centre", n_centre)))
    copies = spread("centre", n_centre, node_ref, points_ref, sem_a.at[0], sem_a.at[1], True)
    copies += spread("node", n_node, centre_ref, centres_ref, sem_b.at[0], sem_b.at[1], True)
    copies += spread("node", n_node, coef_ref, coeffs_ref, sem_c.at[0], sem_c.at[1], True)
    copies += spread("node", n_node, send_ref, recv_ref, sem_d.at[0], sem_d.at[1], False)
    me_node, me_centre = lax.axis_index("node"), lax.axis_index("centre")
    points_ref[me_centre] = node_ref[...]
    centres_ref[me_node] = centre_ref[...]
    coeffs_ref[me_node] = coef_ref[...]
    recv_ref[me_node] = send_ref[me_node]
    for copy in copies:
        copy.wait()


def factor_rows(ref, coords, lanes, left):
    high, rest = split(coords)
    middle, low = split(rest)
    square = jnp.sum(coords * coords, axis=0, keepdims=True)
    scale = 1.0 if left else -2.0
    high, middle, low = high * scale, middle * scale, low * scale
    order = (high, high, middle, middle, high, low) if left else (high, middle, high, middle, low, high)
    for i, piece in enumerate(order):
        ref[3 * i : 3 * i + 3, lanes] = piece
    s_high, s_rest = split(square)
    s_middle, s_low = split(s_rest)
    base = 18 if left else 21
    for i, piece in enumerate((s_high, s_middle, s_low)):
        ref[base + i : base + i + 1, lanes] = piece
    base = 21 if left else 18
    ref[base : base + 3, lanes] = jnp.ones((3, square.shape[1]), F32)


def pair_kernel(
    n_node, n_centre, rows, radius, points_ref, centres_ref, coeffs_ref, recv_ref, index_ref,
    disp_ref, total_ref,
    wide_ref, left_ref, right_ref, coef_ref, force_ref, acc_ref, facc_ref, dacc_ref,
):
    node_part = points_ref.shape[2]
    node_dev = node_part * n_centre
    centre_part = centres_ref.shape[2]
    centre_dev = centre_part * n_node
    node_rows = node_dev // LANES
    capacity = rows * LANES
    inverse = 1.0 / radius
    for o in range(n_node):
        values = []
        for c in range(3):
            row = jnp.concatenate(
                [recv_ref[o, c * rows + r : c * rows + r + 1, :] for r in range(rows)], axis=1
            )
            values.append(split(row))
        values = [v[0] for v in values] + [v[1] for v in values]
        part = scatter_part(values, index_ref[:, o * capacity : (o + 1) * capacity], node_rows)
        if o == 0:
            acc_ref[...] = part
        else:
            acc_ref[...] += part
    force_ref[...] = jnp.zeros_like(force_ref)
    for h in range(node_rows):
        lanes = slice(h * LANES, (h + 1) * LANES)
        piece = acc_ref[pl.ds(h, 6, stride=node_rows), :] * 4.0
        force_ref[0:6, lanes] = piece
    wide_ref[...] = jnp.zeros_like(wide_ref)
    for z in range(n_centre):
        lanes = slice(z * node_part, (z + 1) * node_part)
        factor_rows(wide_ref, (points_ref[z] - 0.5) * inverse, lanes, True)
    for start in range(0, node_dev, 512):
        left_ref[start : start + 512, :] = jnp.transpose(wide_ref[:, start : start + 512]).astype(BF16)
    wide_ref[...] = jnp.zeros_like(wide_ref)
    for o in range(n_node):
        lanes = slice(o * centre_part, (o + 1) * centre_part)
        factor_rows(wide_ref, (centres_ref[o] - 0.5) * inverse, lanes, False)
    right_ref[...] = wide_ref[...].astype(BF16)
    wide_ref[...] = jnp.zeros_like(wide_ref)
    for o in range(n_node):
        lanes = slice(o * centre_part, (o + 1) * centre_part)
        high, low = split(coeffs_ref[o] * 4.0)
        wide_ref[0:6, lanes] = high
        wide_ref[8:14, lanes] = low
    for start in range(0, centre_dev, 512):
        coef_ref[start : start + 512, :] = jnp.transpose(wide_ref[:, start : start + 512]).astype(BF16)
    facc_ref[...] = jnp.zeros_like(facc_ref)
    tile_g, tile_j = min(256, node_dev), min(512, centre_dev)

    @pl.loop(0, node_dev // tile_g)
    def _(i):
        at = pl.ds(pl.multiple_of(i * tile_g, tile_g), tile_g)
        left = left_ref[at, :]
        force = force_ref[:, at].astype(BF16)
        disp = jnp.zeros((tile_g, LANES), F32)
        for start in range(0, centre_dev, tile_j):
            columns = slice(start, start + tile_j)
            squared = jnp.dot(left, right_ref[:, columns], preferred_element_type=F32)
            squared = jnp.maximum(squared, 1e-20)
            scaled = squared * lax.rsqrt(squared)
            remain = jnp.maximum(1.0 - scaled, 0.0)
            remain = remain * remain
            remain = remain * remain
            basis = remain * (scaled + 0.25)
            high = basis.astype(BF16)
            low = (basis - high.astype(F32)).astype(BF16)
            weights = coef_ref[columns, :]
            disp = disp + jnp.dot(high, weights, preferred_element_type=F32)
            disp = disp + jnp.dot(low, weights, preferred_element_type=F32)
            facc_ref[:, columns] += jnp.dot(force, high, preferred_element_type=F32) + jnp.dot(
                force, low, preferred_element_type=F32
            )
        dacc_ref[at, :] = disp

    part_rows = node_part // LANES
    for z in range(n_centre):
        for r in range(part_rows):
            start = z * node_part + r * LANES
            turned = jnp.transpose(dacc_ref[start : start + LANES, :])
            disp_ref[z, pl.ds(r, 6, stride=part_rows), :] = turned[0:6] + turned[8:14]
    for o in range(n_node):
        lanes = slice(o * centre_part, (o + 1) * centre_part)
        total_ref[o] = facc_ref[0:3, lanes] + facc_ref[3:6, lanes]


def reduce_kernel(
    n_node, n_centre, disp_ref, total_ref, whole_ref, force_ref,
    got_disp, got_force, mine_ref, sem_a, sem_b, sem_c,
):
    greet((("node", n_node), ("centre", n_centre)))
    me_node, me_centre = lax.axis_index("node"), lax.axis_index("centre")
    copies = spread("centre", n_centre, disp_ref, got_disp, sem_a.at[0], sem_a.at[1], False)
    later = spread("node", n_node, total_ref, got_force, sem_b.at[0], sem_b.at[1], False)
    got_disp[me_centre] = disp_ref[me_centre]
    got_force[me_node] = total_ref[me_node]
    for copy in copies:
        copy.wait()
    total = got_disp[0]
    for z in range(1, n_centre):
        total = total + got_disp[z]
    mine_ref[...] = total
    whole_ref[me_centre] = total
    copies = spread("centre", n_centre, mine_ref, whole_ref, sem_c.at[0], sem_c.at[1], True)
    for copy in later:
        copy.wait()
    total = got_force[0]
    for o in range(1, n_node):
        total = total + got_force[o]
    force_ref[...] = total
    for copy in copies:
        copy.wait()


def pick_kernel(n_node, n_centre, rows, whole_ref, index_ref, send_ref, tab_ref):
    part_rows = whole_ref.shape[1] // 6
    node_rows = part_rows * n_centre
    capacity = rows * LANES
    lhs = []
    for c in range(6):
        for z in range(n_centre):
            high, low = split(whole_ref[z, c * part_rows : (c + 1) * part_rows, :])
            tab_ref[z * part_rows : (z + 1) * part_rows, :] = high
            tab_ref[node_rows + z * part_rows : node_rows + (z + 1) * part_rows, :] = low
        lhs.append(jnp.transpose(tab_ref[...]).astype(BF16)[:, : 2 * node_rows])
    lhs = jnp.concatenate(lhs, axis=0)
    for o in range(n_node):
        got = gather_part(lhs, index_ref[:, o * capacity : (o + 1) * capacity], node_rows, 6)
        for r in range(rows):
            send_ref[o, pl.ds(r, 6, stride=rows), :] = got[:, r * LANES : (r + 1) * LANES]


def exchange_kernel(n_node, send_ref, recv_ref, sems):
    greet((("node", n_node),))
    copies = spread("node", n_node, send_ref, recv_ref, sems.at[0], sems.at[1], False)
    me = lax.axis_index("node")
    recv_ref[me] = send_ref[me]
    for copy in copies:
        copy.wait()


def place_kernel(n_node, rows, recv_ref, perm_ref, out_ref, tab_ref):
    high_rows = n_node * rows
    lhs = []
    for c in range(6):
        for o in range(n_node):
            high, low = split(recv_ref[o, c * rows : (c + 1) * rows, :])
            tab_ref[o * rows : (o + 1) * rows, :] = high
            tab_ref[high_rows + o * rows : high_rows + (o + 1) * rows, :] = low
        lhs.append(jnp.transpose(tab_ref[...]).astype(BF16))
    lhs = jnp.concatenate(lhs, axis=0)
    fluid_dev = perm_ref.shape[1]
    step = 1024
    for start in range(0, fluid_dev, step):
        out_ref[:, start : start + step] = gather_part(
            lhs, perm_ref[:, start : start + step], high_rows, 6
        )


def body(node_coords, centre_coords, disp_coef, send_count, send_order, slot_perm, fluid_force):
    n_node = lax.axis_size("node")
    n_centre = lax.axis_size("centre")
    node_dev = send_order.shape[1]
    fluid_dev = slot_perm.shape[1]
    capacity = fluid_dev // n_node
    rows = capacity // LANES
    node_rows = node_dev // LANES
    centre_part = centre_coords.shape[1]
    centre_total = centre_part * n_node * n_centre
    centre_dev = centre_part * n_node
    node_part = node_coords.shape[1]
    part_rows = node_part // LANES
    radius = (0.75 * SUPPORT / (math.pi * centre_total)) ** (1.0 / 3.0)
    dma = pltpu.SemaphoreType.DMA
    shape = jax.ShapeDtypeStruct

    def local(function, outs, n_in, scratch, name, specs=None):
        return pl.pallas_call(
            function,
            out_shape=outs,
            in_specs=specs or [vmem()] * n_in,
            out_specs=jax.tree.map(lambda _: vmem(), outs),
            scratch_shapes=scratch,
            name=name,
            compiler_params=pltpu.CompilerParams(vmem_limit_bytes=VMEM_BYTES),
        )

    def remote(function, outs, n_in, scratch, name, number):
        return pl.pallas_call(
            function,
            out_shape=outs,
            in_specs=[vmem()] * n_in,
            out_specs=jax.tree.map(lambda _: vmem(), outs),
            scratch_shapes=scratch,
            name=name,
            compiler_params=pltpu.CompilerParams(
                vmem_limit_bytes=VMEM_BYTES, collective_id=number, has_side_effects=True
            ),
        )

    sent, index = local(
        functools.partial(prepare_kernel, n_node, rows),
        (shape((n_node, 3 * rows, LANES), F32), shape((1, fluid_dev), jnp.int32)),
        4,
        [pltpu.VMEM((6 * fluid_dev // LANES, LANES), F32)],
        "prepare",
        [smem(), vmem(), vmem(), vmem()],
    )(send_count, send_order.reshape(node_rows, LANES), slot_perm, fluid_force)
    points, centres, coeffs, got = remote(
        functools.partial(gather_kernel, n_node, n_centre),
        (
            shape((n_centre, 3, node_part), F32),
            shape((n_node, 3, centre_part), F32),
            shape((n_node, 6, centre_part), F32),
            shape((n_node, 3 * rows, LANES), F32),
        ),
        4,
        [dma((2, n_centre)), dma((2, n_node)), dma((2, n_node)), dma((2, n_node))],
        "gather",
        0,
    )(node_coords, centre_coords, disp_coef, sent)
    partial, totals = local(
        functools.partial(pair_kernel, n_node, n_centre, rows, radius),
        (shape((n_centre, 6 * part_rows, LANES), F32), shape((n_node, 3, centre_part), F32)),
        5,
        [
            pltpu.VMEM((LANES, max(node_dev, centre_dev)), F32),
            pltpu.VMEM((node_dev, LANES), BF16),
            pltpu.VMEM((LANES, centre_dev), BF16),
            pltpu.VMEM((centre_dev, LANES), BF16),
            pltpu.VMEM((16, node_dev), F32),
            pltpu.VMEM((6 * node_rows, LANES), F32),
            pltpu.VMEM((16, centre_dev), F32),
            pltpu.VMEM((node_dev, LANES), F32),
        ],
        "pairs",
    )(points, centres, coeffs, got, index)
    whole, centre_force = remote(
        functools.partial(reduce_kernel, n_node, n_centre),
        (shape((n_centre, 6 * part_rows, LANES), F32), shape((3, centre_part), F32)),
        2,
        [
            pltpu.VMEM((n_centre, 6 * part_rows, LANES), F32),
            pltpu.VMEM((n_node, 3, centre_part), F32),
            pltpu.VMEM((6 * part_rows, LANES), F32),
            dma((2, n_centre)),
            dma((2, n_node)),
            dma((2, n_centre)),
        ],
        "reduce",
        1,
    )(partial, totals)
    outgoing = local(
        functools.partial(pick_kernel, n_node, n_centre, rows),
        shape((n_node, 6 * rows, LANES), F32),
        2,
        [pltpu.VMEM((LANES, LANES), F32)],
        "pick",
    )(whole, index)
    received = remote(
        functools.partial(exchange_kernel, n_node),
        shape((n_node, 6 * rows, LANES), F32),
        1,
        [dma((2, n_node))],
        "exchange",
        2,
    )(outgoing)
    fluid_disp = local(
        functools.partial(place_kernel, n_node, rows),
        shape((6, fluid_dev), F32),
        2,
        [pltpu.VMEM((LANES, LANES), F32)],
        "place",
    )(received, slot_perm)
    return (fluid_disp, centre_force)


def solution(mesh):
    placed = (
        P(None, ("node", "centre")),
        P(None, ("centre", "node")),
        P(None, ("centre", "node")),
        P("node", None),
        P("node", None),
        P("node", None),
        P(None, "node"),
    )
    return jax.shard_map(
        body,
        mesh=mesh,
        in_specs=placed,
        out_specs=(P(None, "node"), P(None, ("centre", "node"))),
        check_vma=False,
    )
```

```python
import functools
import math

import jax
import jax.numpy as jnp
from jax import lax
from jax.experimental import pallas as pl
from jax.experimental.pallas import tpu as pltpu
from jax.sharding import PartitionSpec as P

SUPPORT = 192
LANES = 128
F32 = jnp.float32
BF16 = jnp.bfloat16
VMEM_BYTES = 48 * 1024 * 1024
NT = (((1,), (1,)), ((), ()))


def vmem():
    return pl.BlockSpec(memory_space=pltpu.VMEM)


def smem():
    return pl.BlockSpec(memory_space=pltpu.SMEM)


def split(value):
    high = value.astype(BF16).astype(F32)
    return high, value - high


def onehot(index, rows):
    lanes = index.shape[1]
    return jnp.where(lax.broadcasted_iota(jnp.int32, (rows, lanes), 0) == index, 1.0, 0.0)


def scatter_part(values, index, high_rows):
    n = index.shape[1]
    low = jnp.bitwise_and(index, LANES - 1)
    high = lax.shift_right_arithmetic(index, 7)
    low_hot = onehot(low, LANES).astype(BF16)
    mask = lax.broadcasted_iota(jnp.int32, (high_rows, n), 0) == high
    stacked = jnp.concatenate(
        [jnp.where(mask, value, 0.0).astype(BF16) for value in values], axis=0
    )
    return lax.dot_general(stacked, low_hot, NT, preferred_element_type=F32)


def gather_part(lhs, index, high_rows, channels):
    n = index.shape[1]
    low = jnp.bitwise_and(index, LANES - 1)
    high = lax.shift_right_arithmetic(index, 7)
    hot = onehot(high, high_rows).astype(BF16)
    hot = jnp.concatenate([hot, hot], axis=0)
    wide = jnp.dot(lhs, hot, preferred_element_type=F32)
    mask = lax.broadcasted_iota(jnp.int32, (LANES, n), 0) == low
    rows = [
        jnp.sum(
            jnp.where(mask, wide[c * LANES : (c + 1) * LANES], 0.0), axis=0, keepdims=True
        )
        for c in range(channels)
    ]
    return jnp.concatenate(rows, axis=0)


def prepare_kernel(n_node, rows, count_ref, order_ref, perm_ref, force_ref, send_ref, index_ref, acc_ref):
    fluid_dev = perm_ref.shape[1]
    high_rows = fluid_dev // LANES
    node_rows = order_ref.shape[0]
    capacity = rows * LANES
    step = 1024
    for start in range(0, fluid_dev, step):
        values = []
        for c in range(3):
            values.extend(split(force_ref[c : c + 1, start : start + step]))
        part = scatter_part(values, perm_ref[:, start : start + step], high_rows)
        if start == 0:
            acc_ref[...] = part
        else:
            acc_ref[...] += part
    for c in range(3):
        base = 2 * c * high_rows
        for b in range(n_node):
            lo = base + b * rows
            send_ref[b, c * rows : (c + 1) * rows, :] = (
                acc_ref[lo : lo + rows, :]
                + acc_ref[lo + high_rows : lo + high_rows + rows, :]
            )
    high, low = split(order_ref[...].astype(F32))
    lhs = jnp.transpose(
        jnp.concatenate([high, low, jnp.zeros((LANES - 2 * node_rows, LANES), F32)], axis=0)
    ).astype(BF16)[:, : 2 * node_rows]
    offset = jnp.int32(0)
    for o in range(n_node):
        count = count_ref[0, o]
        slot = lax.broadcasted_iota(jnp.int32, (1, capacity), 1)
        place = jnp.minimum(offset + slot, node_rows * LANES - 1)
        found = gather_part(lhs, place, node_rows, 1).astype(jnp.int32)
        found = jnp.where(slot < count, found, -1)
        index_ref[:, o * capacity : (o + 1) * capacity] = found
        offset = offset + count


def greet(axes):
    barrier = pltpu.get_barrier_semaphore()
    total = 0
    for name, size in axes:
        me = lax.axis_index(name)
        for d in range(1, size):
            pl.semaphore_signal(
                barrier, inc=1, device_id={name: lax.rem(me + d, size)},
                device_id_type=pl.DeviceIdType.MESH,
            )
            total += 1
    pl.semaphore_wait(barrier, total)


def spread(name, size, source, target, send_sem, recv_sem, gather):
    me = lax.axis_index(name)
    copies = []
    for d in range(1, size):
        peer = lax.rem(me + d, size)
        copy = pltpu.make_async_remote_copy(
            src_ref=source if gather else source.at[peer],
            dst_ref=target.at[me],
            send_sem=send_sem.at[d],
            recv_sem=recv_sem.at[d],
            device_id={name: peer},
            device_id_type=pl.DeviceIdType.MESH,
        )
        copy.start()
        copies.append(copy)
    return copies


def gather_kernel(
    n_node, n_centre, node_ref, centre_ref, coef_ref, send_ref,
    points_ref, centres_ref, coeffs_ref, recv_ref, sem_a, sem_b, sem_c, sem_d,
):
    greet((("node", n_node), ("centre", n_centre)))
    copies = spread("centre", n_centre, node_ref, points_ref, sem_a.at[0], sem_a.at[1], True)
    copies += spread("node", n_node, centre_ref, centres_ref, sem_b.at[0], sem_b.at[1], True)
    copies += spread("node", n_node, coef_ref, coeffs_ref, sem_c.at[0], sem_c.at[1], True)
    copies += spread("node", n_node, send_ref, recv_ref, sem_d.at[0], sem_d.at[1], False)
    me_node, me_centre = lax.axis_index("node"), lax.axis_index("centre")
    points_ref[me_centre] = node_ref[...]
    centres_ref[me_node] = centre_ref[...]
    coeffs_ref[me_node] = coef_ref[...]
    recv_ref[me_node] = send_ref[me_node]
    for copy in copies:
        copy.wait()


def factor_rows(ref, coords, lanes, left):
    high, rest = split(coords)
    middle, low = split(rest)
    square = jnp.sum(coords * coords, axis=0, keepdims=True)
    scale = 1.0 if left else -2.0
    high, middle, low = high * scale, middle * scale, low * scale
    order = (high, high, middle, middle, high, low) if left else (high, middle, high, middle, low, high)
    for i, piece in enumerate(order):
        ref[3 * i : 3 * i + 3, lanes] = piece
    s_high, s_rest = split(square)
    s_middle, s_low = split(s_rest)
    base = 18 if left else 21
    for i, piece in enumerate((s_high, s_middle, s_low)):
        ref[base + i : base + i + 1, lanes] = piece
    base = 21 if left else 18
    ref[base : base + 3, lanes] = jnp.ones((3, square.shape[1]), F32)


BINS = 32


def table_factor(table):
    rows = table.shape[0]
    high, low = split(table)
    stacked = jnp.concatenate([high, low, jnp.zeros((LANES - 2 * rows, LANES), F32)], axis=0)
    return jnp.transpose(stacked).astype(BF16)[:, : 2 * rows]


def order_by(first, rank_ref):
    count = first.shape[1]
    bins = jnp.minimum((first * BINS).astype(jnp.int32), BINS - 1)
    member = onehot(bins, BINS)
    below = jnp.where(lax.broadcasted_iota(jnp.int32, (BINS, count), 0) > bins, 1.0, 0.0)
    carry = jnp.sum(below, axis=1, keepdims=True)
    chunks = count // LANES
    stacked = jnp.concatenate(
        [member[:, k * LANES : (k + 1) * LANES] for k in range(chunks)], axis=0
    )
    upper = jnp.where(
        lax.broadcasted_iota(jnp.int32, (LANES, LANES), 0)
        <= lax.broadcasted_iota(jnp.int32, (LANES, LANES), 1),
        1.0,
        0.0,
    ).astype(BF16)
    running = jnp.dot(stacked.astype(BF16), upper, preferred_element_type=F32)
    for k in range(chunks):
        part = running[k * BINS : (k + 1) * BINS]
        mine = stacked[k * BINS : (k + 1) * BINS]
        rank_ref[k : k + 1, :] = jnp.sum(mine * (part + carry), axis=0, keepdims=True) - 1.0
        carry = carry + part[:, LANES - 1 : LANES]


def rank_row(rank_ref, first, last):
    return jnp.concatenate([rank_ref[k : k + 1, :] for k in range(first, last)], axis=1).astype(
        jnp.int32
    )


def pair_kernel(
    n_node, n_centre, rows, radius, points_ref, centres_ref, coeffs_ref, recv_ref, index_ref,
    disp_ref, total_ref, place_ref,
    wide_ref, left_ref, right_ref, coef_ref, force_ref, acc_ref, facc_ref, dacc_ref,
    node_rank, centre_rank, node_sorted, centre_sorted, limit_ref,
):
    node_part = points_ref.shape[2]
    node_dev = node_part * n_centre
    centre_part = centres_ref.shape[2]
    centre_dev = centre_part * n_node
    node_rows, centre_rows = node_dev // LANES, centre_dev // LANES
    capacity = rows * LANES
    inverse = 1.0 / radius
    tile_g, tile_j = min(512, node_dev), min(512, centre_dev)
    n_g, n_j = node_dev // tile_g, centre_dev // tile_j
    order_by(jnp.concatenate([points_ref[z][0:1, :] for z in range(n_centre)], axis=1), node_rank)
    order_by(jnp.concatenate([centres_ref[o][0:1, :] for o in range(n_node)], axis=1), centre_rank)

    def thirds(value):
        high, rest = split(value)
        middle, low = split(rest)
        return [piece[c : c + 1] for piece in (high, middle, low) for c in range(3)]

    used = 9 * node_rows
    for z in range(n_centre):
        per = node_part // LANES
        place = rank_row(node_rank, z * per, (z + 1) * per)
        part = scatter_part(thirds(points_ref[z]), place, node_rows)
        acc_ref[0:used, :] = part if z == 0 else acc_ref[0:used, :] + part
    for h in range(node_rows):
        piece = [acc_ref[pl.ds(3 * i * node_rows + h, 3, stride=node_rows), :] for i in range(3)]
        node_sorted[0:3, h * LANES : (h + 1) * LANES] = piece[0] + piece[1] + piece[2]
    used = 21 * centre_rows
    for o in range(n_node):
        per = centre_part // LANES
        place = rank_row(centre_rank, o * per, (o + 1) * per)
        high, low = split(coeffs_ref[o] * 4.0)
        values = thirds(centres_ref[o]) + [p[c : c + 1] for p in (high, low) for c in range(6)]
        part = scatter_part(values, place, centre_rows)
        acc_ref[0:used, :] = part if o == 0 else acc_ref[0:used, :] + part
    wide_ref[...] = jnp.zeros_like(wide_ref)
    for h in range(centre_rows):
        lanes = slice(h * LANES, (h + 1) * LANES)
        piece = [
            acc_ref[pl.ds(3 * i * centre_rows + h, 3, stride=centre_rows), :] for i in range(3)
        ]
        centre_sorted[0:3, lanes] = piece[0] + piece[1] + piece[2]
        wide_ref[0:6, lanes] = acc_ref[pl.ds(9 * centre_rows + h, 6, stride=centre_rows), :]
        wide_ref[8:14, lanes] = acc_ref[pl.ds(15 * centre_rows + h, 6, stride=centre_rows), :]
    for start in range(0, centre_dev, 512):
        coef_ref[start : start + 512, :] = jnp.transpose(wide_ref[:, start : start + 512]).astype(BF16)
    factor = table_factor(node_rank[...])
    used = 6 * node_rows
    for o in range(n_node):
        slots = slice(o * capacity, (o + 1) * capacity)
        index = index_ref[:, slots]
        place = gather_part(factor, index, node_rows, 1).astype(jnp.int32)
        place = jnp.where(index < 0, -1, place)
        place_ref[:, slots] = place
        values = []
        for c in range(3):
            row = jnp.concatenate(
                [recv_ref[o, c * rows + r : c * rows + r + 1, :] for r in range(rows)], axis=1
            )
            values.append(split(row))
        values = [v[0] for v in values] + [v[1] for v in values]
        part = scatter_part(values, place, node_rows)
        acc_ref[0:used, :] = part if o == 0 else acc_ref[0:used, :] + part
    force_ref[...] = jnp.zeros_like(force_ref)
    for h in range(node_rows):
        lanes = slice(h * LANES, (h + 1) * LANES)
        force_ref[0:6, lanes] = acc_ref[pl.ds(h, 6, stride=node_rows), :] * 4.0
    wide_ref[...] = jnp.zeros_like(wide_ref)
    for start in range(0, node_dev, 1024):
        lanes = slice(start, start + 1024)
        factor_rows(wide_ref, (node_sorted[0:3, lanes] - 0.5) * inverse, lanes, True)
    for start in range(0, node_dev, 512):
        left_ref[start : start + 512, :] = jnp.transpose(wide_ref[:, start : start + 512]).astype(BF16)
    wide_ref[...] = jnp.zeros_like(wide_ref)
    for start in range(0, centre_dev, 512):
        lanes = slice(start, start + 512)
        factor_rows(wide_ref, (centre_sorted[0:3, lanes] - 0.5) * inverse, lanes, False)
    right_ref[...] = wide_ref[...].astype(BF16)
    reach = radius * 1.00001
    upto, since = [], []
    for j in range(n_j):
        row = centre_sorted[0:1, j * tile_j : (j + 1) * tile_j]
        upto.append(jnp.max(row))
        since.append(jnp.min(row))
    for j in range(1, n_j):
        upto[j] = jnp.maximum(upto[j], upto[j - 1])
    for j in range(n_j - 2, -1, -1):
        since[j] = jnp.minimum(since[j], since[j + 1])
    for i in range(n_g):
        row = node_sorted[0:1, i * tile_g : (i + 1) * tile_g]
        least, most = jnp.min(row) - reach, jnp.max(row) + reach
        before, after = jnp.int32(0), jnp.int32(n_j)
        for j in range(n_j):
            before = before + jnp.where(upto[j] < least, 1, 0)
            after = after - jnp.where(since[j] > most, 1, 0)
        limit_ref[0, i] = before
        limit_ref[1, i] = after
    facc_ref[...] = jnp.zeros_like(facc_ref)
    dacc_ref[...] = jnp.zeros_like(dacc_ref)

    @pl.loop(0, n_g)
    def _(i):
        at = pl.ds(pl.multiple_of(i * tile_g, tile_g), tile_g)

        @pl.loop(limit_ref[0, i], limit_ref[1, i])
        def _(j):
            columns = pl.ds(pl.multiple_of(j * tile_j, tile_j), tile_j)
            force = force_ref[:, at].astype(BF16)
            squared = jnp.dot(left_ref[at, :], right_ref[:, columns], preferred_element_type=F32)
            squared = jnp.maximum(squared, 1e-20)
            scaled = squared * lax.rsqrt(squared)
            remain = jnp.maximum(1.0 - scaled, 0.0)
            remain = remain * remain
            remain = remain * remain
            basis = remain * (scaled + 0.25)
            high = basis.astype(BF16)
            low = (basis - high.astype(F32)).astype(BF16)
            weights = coef_ref[columns, :]
            dacc_ref[at, :] += jnp.dot(high, weights, preferred_element_type=F32) + jnp.dot(
                low, weights, preferred_element_type=F32
            )
            facc_ref[:, columns] += jnp.dot(force, high, preferred_element_type=F32) + jnp.dot(
                force, low, preferred_element_type=F32
            )

    part_rows = node_part // LANES
    for z in range(n_centre):
        for r in range(part_rows):
            start = z * node_part + r * LANES
            turned = jnp.transpose(dacc_ref[start : start + LANES, :])
            disp_ref[z, pl.ds(r, 6, stride=part_rows), :] = turned[0:6] + turned[8:14]
    for h in range(centre_rows):
        lanes = slice(h * LANES, (h + 1) * LANES)
        acc_ref[pl.ds(h, 3, stride=centre_rows), :] = facc_ref[0:3, lanes] + facc_ref[3:6, lanes]
    factor = jnp.concatenate(
        [table_factor(acc_ref[c * centre_rows : (c + 1) * centre_rows, :]) for c in range(3)],
        axis=0,
    )
    for o in range(n_node):
        per = centre_part // LANES
        place = rank_row(centre_rank, o * per, (o + 1) * per)
        total_ref[o] = gather_part(factor, place, centre_rows, 3)


def reduce_kernel(
    n_node, n_centre, disp_ref, total_ref, whole_ref, force_ref,
    got_disp, got_force, mine_ref, sem_a, sem_b, sem_c,
):
    greet((("node", n_node), ("centre", n_centre)))
    me_node, me_centre = lax.axis_index("node"), lax.axis_index("centre")
    copies = spread("centre", n_centre, disp_ref, got_disp, sem_a.at[0], sem_a.at[1], False)
    later = spread("node", n_node, total_ref, got_force, sem_b.at[0], sem_b.at[1], False)
    got_disp[me_centre] = disp_ref[me_centre]
    got_force[me_node] = total_ref[me_node]
    for copy in copies:
        copy.wait()
    total = got_disp[0]
    for z in range(1, n_centre):
        total = total + got_disp[z]
    mine_ref[...] = total
    whole_ref[me_centre] = total
    copies = spread("centre", n_centre, mine_ref, whole_ref, sem_c.at[0], sem_c.at[1], True)
    for copy in later:
        copy.wait()
    total = got_force[0]
    for o in range(1, n_node):
        total = total + got_force[o]
    force_ref[...] = total
    for copy in copies:
        copy.wait()


def pick_kernel(n_node, n_centre, rows, whole_ref, index_ref, send_ref, tab_ref):
    part_rows = whole_ref.shape[1] // 6
    node_rows = part_rows * n_centre
    capacity = rows * LANES
    lhs = []
    for c in range(6):
        for z in range(n_centre):
            high, low = split(whole_ref[z, c * part_rows : (c + 1) * part_rows, :])
            tab_ref[z * part_rows : (z + 1) * part_rows, :] = high
            tab_ref[node_rows + z * part_rows : node_rows + (z + 1) * part_rows, :] = low
        lhs.append(jnp.transpose(tab_ref[...]).astype(BF16)[:, : 2 * node_rows])
    lhs = jnp.concatenate(lhs, axis=0)
    for o in range(n_node):
        got = gather_part(lhs, index_ref[:, o * capacity : (o + 1) * capacity], node_rows, 6)
        for r in range(rows):
            send_ref[o, pl.ds(r, 6, stride=rows), :] = got[:, r * LANES : (r + 1) * LANES]


def exchange_kernel(n_node, send_ref, recv_ref, sems):
    greet((("node", n_node),))
    copies = spread("node", n_node, send_ref, recv_ref, sems.at[0], sems.at[1], False)
    me = lax.axis_index("node")
    recv_ref[me] = send_ref[me]
    for copy in copies:
        copy.wait()


def place_kernel(n_node, rows, recv_ref, perm_ref, out_ref, tab_ref):
    high_rows = n_node * rows
    lhs = []
    for c in range(6):
        for o in range(n_node):
            high, low = split(recv_ref[o, c * rows : (c + 1) * rows, :])
            tab_ref[o * rows : (o + 1) * rows, :] = high
            tab_ref[high_rows + o * rows : high_rows + (o + 1) * rows, :] = low
        lhs.append(jnp.transpose(tab_ref[...]).astype(BF16))
    lhs = jnp.concatenate(lhs, axis=0)
    fluid_dev = perm_ref.shape[1]
    step = 1024
    for start in range(0, fluid_dev, step):
        out_ref[:, start : start + step] = gather_part(
            lhs, perm_ref[:, start : start + step], high_rows, 6
        )


def body(node_coords, centre_coords, disp_coef, send_count, send_order, slot_perm, fluid_force):
    n_node = lax.axis_size("node")
    n_centre = lax.axis_size("centre")
    node_dev = send_order.shape[1]
    fluid_dev = slot_perm.shape[1]
    capacity = fluid_dev // n_node
    rows = capacity // LANES
    node_rows = node_dev // LANES
    centre_part = centre_coords.shape[1]
    centre_total = centre_part * n_node * n_centre
    centre_dev = centre_part * n_node
    node_part = node_coords.shape[1]
    part_rows = node_part // LANES
    radius = (0.75 * SUPPORT / (math.pi * centre_total)) ** (1.0 / 3.0)
    dma = pltpu.SemaphoreType.DMA
    shape = jax.ShapeDtypeStruct

    def local(function, outs, n_in, scratch, name, specs=None):
        return pl.pallas_call(
            function,
            out_shape=outs,
            in_specs=specs or [vmem()] * n_in,
            out_specs=jax.tree.map(lambda _: vmem(), outs),
            scratch_shapes=scratch,
            name=name,
            compiler_params=pltpu.CompilerParams(vmem_limit_bytes=VMEM_BYTES),
        )

    def remote(function, outs, n_in, scratch, name, number):
        return pl.pallas_call(
            function,
            out_shape=outs,
            in_specs=[vmem()] * n_in,
            out_specs=jax.tree.map(lambda _: vmem(), outs),
            scratch_shapes=scratch,
            name=name,
            compiler_params=pltpu.CompilerParams(
                vmem_limit_bytes=VMEM_BYTES, collective_id=number, has_side_effects=True
            ),
        )

    sent, index = local(
        functools.partial(prepare_kernel, n_node, rows),
        (shape((n_node, 3 * rows, LANES), F32), shape((1, fluid_dev), jnp.int32)),
        4,
        [pltpu.VMEM((6 * fluid_dev // LANES, LANES), F32)],
        "prepare",
        [smem(), vmem(), vmem(), vmem()],
    )(send_count, send_order.reshape(node_rows, LANES), slot_perm, fluid_force)
    points, centres, coeffs, got = remote(
        functools.partial(gather_kernel, n_node, n_centre),
        (
            shape((n_centre, 3, node_part), F32),
            shape((n_node, 3, centre_part), F32),
            shape((n_node, 6, centre_part), F32),
            shape((n_node, 3 * rows, LANES), F32),
        ),
        4,
        [dma((2, n_centre)), dma((2, n_node)), dma((2, n_node)), dma((2, n_node))],
        "gather",
        0,
    )(node_coords, centre_coords, disp_coef, sent)
    partial, totals, places = local(
        functools.partial(pair_kernel, n_node, n_centre, rows, radius),
        (
            shape((n_centre, 6 * part_rows, LANES), F32),
            shape((n_node, 3, centre_part), F32),
            shape((1, fluid_dev), jnp.int32),
        ),
        5,
        [
            pltpu.VMEM((LANES, max(node_dev, centre_dev)), F32),
            pltpu.VMEM((node_dev, LANES), BF16),
            pltpu.VMEM((LANES, centre_dev), BF16),
            pltpu.VMEM((centre_dev, LANES), BF16),
            pltpu.VMEM((16, node_dev), F32),
            pltpu.VMEM((max(9 * node_rows, 21 * centre_dev // LANES), LANES), F32),
            pltpu.VMEM((16, centre_dev), F32),
            pltpu.VMEM((node_dev, LANES), F32),
            pltpu.VMEM((node_rows, LANES), F32),
            pltpu.VMEM((centre_dev // LANES, LANES), F32),
            pltpu.VMEM((8, node_dev), F32),
            pltpu.VMEM((8, centre_dev), F32),
            pltpu.SMEM((2, node_dev // min(512, node_dev)), jnp.int32),
        ],
        "pairs",
    )(points, centres, coeffs, got, index)
    whole, centre_force = remote(
        functools.partial(reduce_kernel, n_node, n_centre),
        (shape((n_centre, 6 * part_rows, LANES), F32), shape((3, centre_part), F32)),
        2,
        [
            pltpu.VMEM((n_centre, 6 * part_rows, LANES), F32),
            pltpu.VMEM((n_node, 3, centre_part), F32),
            pltpu.VMEM((6 * part_rows, LANES), F32),
            dma((2, n_centre)),
            dma((2, n_node)),
            dma((2, n_centre)),
        ],
        "reduce",
        1,
    )(partial, totals)
    outgoing = local(
        functools.partial(pick_kernel, n_node, n_centre, rows),
        shape((n_node, 6 * rows, LANES), F32),
        2,
        [pltpu.VMEM((LANES, LANES), F32)],
        "pick",
    )(whole, places)
    received = remote(
        functools.partial(exchange_kernel, n_node),
        shape((n_node, 6 * rows, LANES), F32),
        1,
        [dma((2, n_node))],
        "exchange",
        2,
    )(outgoing)
    fluid_disp = local(
        functools.partial(place_kernel, n_node, rows),
        shape((6, fluid_dev), F32),
        2,
        [pltpu.VMEM((LANES, LANES), F32)],
        "place",
    )(received, slot_perm)
    return (fluid_disp, centre_force)


def solution(mesh):
    placed = (
        P(None, ("node", "centre")),
        P(None, ("centre", "node")),
        P(None, ("centre", "node")),
        P("node", None),
        P("node", None),
        P("node", None),
        P(None, "node"),
    )
    return jax.shard_map(
        body,
        mesh=mesh,
        in_specs=placed,
        out_specs=(P(None, "node"), P(None, ("centre", "node"))),
        check_vma=False,
    )
```

```python
import functools
import math

import jax
import jax.numpy as jnp
from jax import lax
from jax.experimental import pallas as pl
from jax.experimental.pallas import tpu as pltpu
from jax.sharding import PartitionSpec as P

SUPPORT = 192
LANES = 128
F32 = jnp.float32
BF16 = jnp.bfloat16
VMEM_BYTES = 48 * 1024 * 1024
NT = (((1,), (1,)), ((), ()))


def vmem():
    return pl.BlockSpec(memory_space=pltpu.VMEM)


def smem():
    return pl.BlockSpec(memory_space=pltpu.SMEM)


def split(value):
    high = value.astype(BF16).astype(F32)
    return high, value - high


def onehot(index, rows):
    lanes = index.shape[1]
    return jnp.where(lax.broadcasted_iota(jnp.int32, (rows, lanes), 0) == index, 1.0, 0.0)


def scatter_part(values, index, high_rows):
    n = index.shape[1]
    low = jnp.bitwise_and(index, LANES - 1)
    high = lax.shift_right_arithmetic(index, 7)
    low_hot = onehot(low, LANES).astype(BF16)
    mask = lax.broadcasted_iota(jnp.int32, (high_rows, n), 0) == high
    stacked = jnp.concatenate(
        [jnp.where(mask, value, 0.0).astype(BF16) for value in values], axis=0
    )
    return lax.dot_general(stacked, low_hot, NT, preferred_element_type=F32)


def gather_part(lhs, index, high_rows, channels):
    n = index.shape[1]
    low = jnp.bitwise_and(index, LANES - 1)
    high = lax.shift_right_arithmetic(index, 7)
    hot = onehot(high, high_rows).astype(BF16)
    hot = jnp.concatenate([hot, hot], axis=0)
    wide = jnp.dot(lhs, hot, preferred_element_type=F32)
    mask = lax.broadcasted_iota(jnp.int32, (LANES, n), 0) == low
    rows = [
        jnp.sum(
            jnp.where(mask, wide[c * LANES : (c + 1) * LANES], 0.0), axis=0, keepdims=True
        )
        for c in range(channels)
    ]
    return jnp.concatenate(rows, axis=0)


def fill_slots(n_node, rows, perm_ref, force_ref, send_ref, acc_ref):
    fluid_dev = perm_ref.shape[1]
    high_rows = fluid_dev // LANES
    step = 1024
    for start in range(0, fluid_dev, step):
        values = []
        for c in range(3):
            values.extend(split(force_ref[c : c + 1, start : start + step]))
        part = scatter_part(values, perm_ref[:, start : start + step], high_rows)
        if start == 0:
            acc_ref[...] = part
        else:
            acc_ref[...] += part
    for c in range(3):
        base = 2 * c * high_rows
        for b in range(n_node):
            lo = base + b * rows
            send_ref[b, c * rows : (c + 1) * rows, :] = (
                acc_ref[lo : lo + rows, :]
                + acc_ref[lo + high_rows : lo + high_rows + rows, :]
            )


def find_nodes(n_node, rows, count_ref, order_ref, index_ref):
    node_rows = order_ref.shape[0]
    capacity = rows * LANES
    high, low = split(order_ref[...].astype(F32))
    lhs = jnp.transpose(
        jnp.concatenate([high, low, jnp.zeros((LANES - 2 * node_rows, LANES), F32)], axis=0)
    ).astype(BF16)[:, : 2 * node_rows]
    offset = jnp.int32(0)
    for o in range(n_node):
        count = count_ref[0, o]
        slot = lax.broadcasted_iota(jnp.int32, (1, capacity), 1)
        place = jnp.minimum(offset + slot, node_rows * LANES - 1)
        found = gather_part(lhs, place, node_rows, 1).astype(jnp.int32)
        found = jnp.where(slot < count, found, -1)
        index_ref[:, o * capacity : (o + 1) * capacity] = found
        offset = offset + count


def greet(axes):
    barrier = pltpu.get_barrier_semaphore()
    total = 0
    for name, size in axes:
        me = lax.axis_index(name)
        for d in range(1, size):
            pl.semaphore_signal(
                barrier, inc=1, device_id={name: lax.rem(me + d, size)},
                device_id_type=pl.DeviceIdType.MESH,
            )
            total += 1
    pl.semaphore_wait(barrier, total)


def spread(name, size, source, target, send_sem, recv_sem, gather):
    me = lax.axis_index(name)
    copies = []
    for d in range(1, size):
        peer = lax.rem(me + d, size)
        copy = pltpu.make_async_remote_copy(
            src_ref=source if gather else source.at[peer],
            dst_ref=target.at[me],
            send_sem=send_sem.at[d],
            recv_sem=recv_sem.at[d],
            device_id={name: peer},
            device_id_type=pl.DeviceIdType.MESH,
        )
        copy.start()
        copies.append(copy)
    return copies


def gather_kernel(
    n_node, n_centre, rows, node_ref, centre_ref, coef_ref, count_ref, order_in, perm_in, force_in,
    points_ref, centres_ref, coeffs_ref, recv_ref, index_ref,
    order_ref, perm_ref, force_ref, send_ref, acc_ref, sem_a, sem_b, sem_c, sem_d, sem_in,
):
    loads = [
        pltpu.make_async_copy(perm_in, perm_ref, sem_in.at[0]),
        pltpu.make_async_copy(force_in, force_ref, sem_in.at[1]),
        pltpu.make_async_copy(order_in, order_ref, sem_in.at[2]),
    ]
    for load in loads:
        load.start()
    greet((("node", n_node), ("centre", n_centre)))
    copies = spread("centre", n_centre, node_ref, points_ref, sem_a.at[0], sem_a.at[1], True)
    copies += spread("node", n_node, centre_ref, centres_ref, sem_b.at[0], sem_b.at[1], True)
    copies += spread("node", n_node, coef_ref, coeffs_ref, sem_c.at[0], sem_c.at[1], True)
    for load in loads:
        load.wait()
    fill_slots(n_node, rows, perm_ref, force_ref, send_ref, acc_ref)
    copies += spread("node", n_node, send_ref, recv_ref, sem_d.at[0], sem_d.at[1], False)
    me_node, me_centre = lax.axis_index("node"), lax.axis_index("centre")
    points_ref[me_centre] = node_ref[...]
    centres_ref[me_node] = centre_ref[...]
    coeffs_ref[me_node] = coef_ref[...]
    recv_ref[me_node] = send_ref[me_node]
    find_nodes(n_node, rows, count_ref, order_ref, index_ref)
    for copy in copies:
        copy.wait()


def factor_rows(ref, coords, lanes, left):
    high, rest = split(coords)
    middle, low = split(rest)
    square = jnp.sum(coords * coords, axis=0, keepdims=True)
    scale = 1.0 if left else -2.0
    high, middle, low = high * scale, middle * scale, low * scale
    order = (high, high, middle, middle, high, low) if left else (high, middle, high, middle, low, high)
    for i, piece in enumerate(order):
        ref[3 * i : 3 * i + 3, lanes] = piece
    s_high, s_rest = split(square)
    s_middle, s_low = split(s_rest)
    base = 18 if left else 21
    for i, piece in enumerate((s_high, s_middle, s_low)):
        ref[base + i : base + i + 1, lanes] = piece
    base = 21 if left else 18
    ref[base : base + 3, lanes] = jnp.ones((3, square.shape[1]), F32)


BINS = 32


def table_factor(table):
    rows = table.shape[0]
    high, low = split(table)
    stacked = jnp.concatenate([high, low, jnp.zeros((LANES - 2 * rows, LANES), F32)], axis=0)
    return jnp.transpose(stacked).astype(BF16)[:, : 2 * rows]


def order_by(first, rank_ref):
    count = first.shape[1]
    bins = jnp.minimum((first * BINS).astype(jnp.int32), BINS - 1)
    member = onehot(bins, BINS)
    below = jnp.where(lax.broadcasted_iota(jnp.int32, (BINS, count), 0) > bins, 1.0, 0.0)
    carry = jnp.sum(below, axis=1, keepdims=True)
    chunks = count // LANES
    stacked = jnp.concatenate(
        [member[:, k * LANES : (k + 1) * LANES] for k in range(chunks)], axis=0
    )
    upper = jnp.where(
        lax.broadcasted_iota(jnp.int32, (LANES, LANES), 0)
        <= lax.broadcasted_iota(jnp.int32, (LANES, LANES), 1),
        1.0,
        0.0,
    ).astype(BF16)
    running = jnp.dot(stacked.astype(BF16), upper, preferred_element_type=F32)
    for k in range(chunks):
        part = running[k * BINS : (k + 1) * BINS]
        mine = stacked[k * BINS : (k + 1) * BINS]
        rank_ref[k : k + 1, :] = jnp.sum(mine * (part + carry), axis=0, keepdims=True) - 1.0
        carry = carry + part[:, LANES - 1 : LANES]


def rank_row(rank_ref, first, last):
    return jnp.concatenate([rank_ref[k : k + 1, :] for k in range(first, last)], axis=1).astype(
        jnp.int32
    )


def pair_kernel(
    n_node, n_centre, rows, radius, points_ref, centres_ref, coeffs_ref, recv_ref, index_ref,
    disp_ref, total_ref, place_ref,
    wide_ref, left_ref, right_ref, coef_ref, force_ref, acc_ref, facc_ref, dacc_ref,
    node_rank, centre_rank, node_sorted, centre_sorted, limit_ref,
):
    node_part = points_ref.shape[2]
    node_dev = node_part * n_centre
    centre_part = centres_ref.shape[2]
    centre_dev = centre_part * n_node
    node_rows, centre_rows = node_dev // LANES, centre_dev // LANES
    capacity = rows * LANES
    inverse = 1.0 / radius
    tile_g, tile_j = min(512, node_dev), min(512, centre_dev)
    n_g, n_j = node_dev // tile_g, centre_dev // tile_j
    order_by(jnp.concatenate([points_ref[z][0:1, :] for z in range(n_centre)], axis=1), node_rank)
    order_by(jnp.concatenate([centres_ref[o][0:1, :] for o in range(n_node)], axis=1), centre_rank)

    def thirds(value):
        high, rest = split(value)
        middle, low = split(rest)
        return [piece[c : c + 1] for piece in (high, middle, low) for c in range(3)]

    used = 9 * node_rows
    for z in range(n_centre):
        per = node_part // LANES
        place = rank_row(node_rank, z * per, (z + 1) * per)
        part = scatter_part(thirds(points_ref[z]), place, node_rows)
        acc_ref[0:used, :] = part if z == 0 else acc_ref[0:used, :] + part
    for h in range(node_rows):
        piece = [acc_ref[pl.ds(3 * i * node_rows + h, 3, stride=node_rows), :] for i in range(3)]
        node_sorted[0:3, h * LANES : (h + 1) * LANES] = piece[0] + piece[1] + piece[2]
    used = 21 * centre_rows
    for o in range(n_node):
        per = centre_part // LANES
        place = rank_row(centre_rank, o * per, (o + 1) * per)
        high, low = split(coeffs_ref[o] * 4.0)
        values = thirds(centres_ref[o]) + [p[c : c + 1] for p in (high, low) for c in range(6)]
        part = scatter_part(values, place, centre_rows)
        acc_ref[0:used, :] = part if o == 0 else acc_ref[0:used, :] + part
    wide_ref[...] = jnp.zeros_like(wide_ref)
    for h in range(centre_rows):
        lanes = slice(h * LANES, (h + 1) * LANES)
        piece = [
            acc_ref[pl.ds(3 * i * centre_rows + h, 3, stride=centre_rows), :] for i in range(3)
        ]
        centre_sorted[0:3, lanes] = piece[0] + piece[1] + piece[2]
        wide_ref[0:6, lanes] = acc_ref[pl.ds(9 * centre_rows + h, 6, stride=centre_rows), :]
        wide_ref[8:14, lanes] = acc_ref[pl.ds(15 * centre_rows + h, 6, stride=centre_rows), :]
    for start in range(0, centre_dev, 512):
        coef_ref[start : start + 512, :] = jnp.transpose(wide_ref[:, start : start + 512]).astype(BF16)
    factor = table_factor(node_rank[...])
    used = 6 * node_rows
    for o in range(n_node):
        slots = slice(o * capacity, (o + 1) * capacity)
        index = index_ref[:, slots]
        place = gather_part(factor, index, node_rows, 1).astype(jnp.int32)
        place = jnp.where(index < 0, -1, place)
        place_ref[:, slots] = place
        values = []
        for c in range(3):
            row = jnp.concatenate(
                [recv_ref[o, c * rows + r : c * rows + r + 1, :] for r in range(rows)], axis=1
            )
            values.append(split(row))
        values = [v[0] for v in values] + [v[1] for v in values]
        part = scatter_part(values, place, node_rows)
        acc_ref[0:used, :] = part if o == 0 else acc_ref[0:used, :] + part
    force_ref[...] = jnp.zeros_like(force_ref)
    for h in range(node_rows):
        lanes = slice(h * LANES, (h + 1) * LANES)
        force_ref[0:6, lanes] = acc_ref[pl.ds(h, 6, stride=node_rows), :] * 4.0
    wide_ref[...] = jnp.zeros_like(wide_ref)
    for start in range(0, node_dev, 1024):
        lanes = slice(start, start + 1024)
        factor_rows(wide_ref, (node_sorted[0:3, lanes] - 0.5) * inverse, lanes, True)
    for start in range(0, node_dev, 512):
        left_ref[start : start + 512, :] = jnp.transpose(wide_ref[:, start : start + 512]).astype(BF16)
    wide_ref[...] = jnp.zeros_like(wide_ref)
    for start in range(0, centre_dev, 512):
        lanes = slice(start, start + 512)
        factor_rows(wide_ref, (centre_sorted[0:3, lanes] - 0.5) * inverse, lanes, False)
    right_ref[...] = wide_ref[...].astype(BF16)
    reach = radius * 1.00001
    upto, since = [], []
    for j in range(n_j):
        row = centre_sorted[0:1, j * tile_j : (j + 1) * tile_j]
        upto.append(jnp.max(row))
        since.append(jnp.min(row))
    for j in range(1, n_j):
        upto[j] = jnp.maximum(upto[j], upto[j - 1])
    for j in range(n_j - 2, -1, -1):
        since[j] = jnp.minimum(since[j], since[j + 1])
    for i in range(n_g):
        row = node_sorted[0:1, i * tile_g : (i + 1) * tile_g]
        least, most = jnp.min(row) - reach, jnp.max(row) + reach
        before, after = jnp.int32(0), jnp.int32(n_j)
        for j in range(n_j):
            before = before + jnp.where(upto[j] < least, 1, 0)
            after = after - jnp.where(since[j] > most, 1, 0)
        limit_ref[0, i] = before
        limit_ref[1, i] = after
    facc_ref[...] = jnp.zeros_like(facc_ref)
    dacc_ref[...] = jnp.zeros_like(dacc_ref)

    @pl.loop(0, n_g)
    def _(i):
        at = pl.ds(pl.multiple_of(i * tile_g, tile_g), tile_g)

        @pl.loop(limit_ref[0, i], limit_ref[1, i])
        def _(j):
            columns = pl.ds(pl.multiple_of(j * tile_j, tile_j), tile_j)
            force = force_ref[:, at].astype(BF16)
            squared = jnp.dot(left_ref[at, :], right_ref[:, columns], preferred_element_type=F32)
            squared = jnp.maximum(squared, 1e-20)
            scaled = squared * lax.rsqrt(squared)
            remain = jnp.maximum(1.0 - scaled, 0.0)
            remain = remain * remain
            remain = remain * remain
            basis = remain * (scaled + 0.25)
            high = basis.astype(BF16)
            low = (basis - high.astype(F32)).astype(BF16)
            weights = coef_ref[columns, :]
            dacc_ref[at, :] += jnp.dot(high, weights, preferred_element_type=F32) + jnp.dot(
                low, weights, preferred_element_type=F32
            )
            facc_ref[:, columns] += jnp.dot(force, high, preferred_element_type=F32) + jnp.dot(
                force, low, preferred_element_type=F32
            )

    part_rows = node_part // LANES
    for z in range(n_centre):
        for r in range(part_rows):
            start = z * node_part + r * LANES
            turned = jnp.transpose(dacc_ref[start : start + LANES, :])
            disp_ref[z, pl.ds(r, 6, stride=part_rows), :] = turned[0:6] + turned[8:14]
    for h in range(centre_rows):
        lanes = slice(h * LANES, (h + 1) * LANES)
        acc_ref[pl.ds(h, 3, stride=centre_rows), :] = facc_ref[0:3, lanes] + facc_ref[3:6, lanes]
    factor = jnp.concatenate(
        [table_factor(acc_ref[c * centre_rows : (c + 1) * centre_rows, :]) for c in range(3)],
        axis=0,
    )
    for o in range(n_node):
        per = centre_part // LANES
        place = rank_row(centre_rank, o * per, (o + 1) * per)
        total_ref[o] = gather_part(factor, place, centre_rows, 3)


def reduce_kernel(
    n_node, n_centre, rows, disp_ref, total_ref, index_ref, recv_ref, force_ref,
    got_disp, got_force, mine_ref, whole_ref, send_ref, tab_ref, sem_a, sem_b, sem_c, sem_d,
):
    greet((("node", n_node), ("centre", n_centre)))
    me_node, me_centre = lax.axis_index("node"), lax.axis_index("centre")
    copies = spread("centre", n_centre, disp_ref, got_disp, sem_a.at[0], sem_a.at[1], False)
    later = spread("node", n_node, total_ref, got_force, sem_b.at[0], sem_b.at[1], False)
    got_disp[me_centre] = disp_ref[me_centre]
    got_force[me_node] = total_ref[me_node]
    for copy in copies:
        copy.wait()
    total = got_disp[0]
    for z in range(1, n_centre):
        total = total + got_disp[z]
    mine_ref[...] = total
    whole_ref[me_centre] = total
    copies = spread("centre", n_centre, mine_ref, whole_ref, sem_c.at[0], sem_c.at[1], True)
    for copy in later:
        copy.wait()
    total = got_force[0]
    for o in range(1, n_node):
        total = total + got_force[o]
    force_ref[...] = total
    for copy in copies:
        copy.wait()
    part_rows = whole_ref.shape[1] // 6
    node_rows = part_rows * n_centre
    capacity = rows * LANES
    factor = []
    for c in range(6):
        for z in range(n_centre):
            tab_ref[z * part_rows : (z + 1) * part_rows, :] = whole_ref[
                z, c * part_rows : (c + 1) * part_rows, :
            ]
        factor.append(table_factor(tab_ref[...]))
    factor = jnp.concatenate(factor, axis=0)
    copies = []
    for d in list(range(1, n_node)) + [0]:
        peer = lax.rem(me_node + d, n_node)
        slots = pl.ds(pl.multiple_of(peer * capacity, LANES), capacity)
        got = gather_part(factor, index_ref[:, slots], node_rows, 6)
        for r in range(rows):
            send_ref[d, pl.ds(r, 6, stride=rows), :] = got[:, r * LANES : (r + 1) * LANES]
        if d == 0:
            continue
        copy = pltpu.make_async_remote_copy(
            src_ref=send_ref.at[d],
            dst_ref=recv_ref.at[me_node],
            send_sem=sem_d.at[0, d],
            recv_sem=sem_d.at[1, d],
            device_id={"node": peer},
            device_id_type=pl.DeviceIdType.MESH,
        )
        copy.start()
        copies.append(copy)
    recv_ref[me_node] = send_ref[0]
    for copy in copies:
        copy.wait()


def place_kernel(n_node, rows, recv_ref, perm_ref, out_ref, tab_ref):
    high_rows = n_node * rows
    lhs = []
    for c in range(6):
        for o in range(n_node):
            high, low = split(recv_ref[o, c * rows : (c + 1) * rows, :])
            tab_ref[o * rows : (o + 1) * rows, :] = high
            tab_ref[high_rows + o * rows : high_rows + (o + 1) * rows, :] = low
        lhs.append(jnp.transpose(tab_ref[...]).astype(BF16))
    lhs = jnp.concatenate(lhs, axis=0)
    fluid_dev = perm_ref.shape[1]
    step = 1024
    for start in range(0, fluid_dev, step):
        out_ref[:, start : start + step] = gather_part(
            lhs, perm_ref[:, start : start + step], high_rows, 6
        )


def body(node_coords, centre_coords, disp_coef, send_count, send_order, slot_perm, fluid_force):
    n_node = lax.axis_size("node")
    n_centre = lax.axis_size("centre")
    node_dev = send_order.shape[1]
    fluid_dev = slot_perm.shape[1]
    capacity = fluid_dev // n_node
    rows = capacity // LANES
    node_rows = node_dev // LANES
    centre_part = centre_coords.shape[1]
    centre_total = centre_part * n_node * n_centre
    centre_dev = centre_part * n_node
    node_part = node_coords.shape[1]
    part_rows = node_part // LANES
    radius = (0.75 * SUPPORT / (math.pi * centre_total)) ** (1.0 / 3.0)
    dma = pltpu.SemaphoreType.DMA
    shape = jax.ShapeDtypeStruct

    def local(function, outs, n_in, scratch, name, specs=None):
        return pl.pallas_call(
            function,
            out_shape=outs,
            in_specs=specs or [vmem()] * n_in,
            out_specs=jax.tree.map(lambda _: vmem(), outs),
            scratch_shapes=scratch,
            name=name,
            compiler_params=pltpu.CompilerParams(vmem_limit_bytes=VMEM_BYTES),
        )

    def remote(function, outs, n_in, scratch, name, number, specs=None):
        return pl.pallas_call(
            function,
            out_shape=outs,
            in_specs=specs or [vmem()] * n_in,
            out_specs=jax.tree.map(lambda _: vmem(), outs),
            scratch_shapes=scratch,
            name=name,
            compiler_params=pltpu.CompilerParams(
                vmem_limit_bytes=VMEM_BYTES, collective_id=number, has_side_effects=True
            ),
        )

    anywhere = pl.BlockSpec(memory_space=pl.ANY)
    points, centres, coeffs, got, index = remote(
        functools.partial(gather_kernel, n_node, n_centre, rows),
        (
            shape((n_centre, 3, node_part), F32),
            shape((n_node, 3, centre_part), F32),
            shape((n_node, 6, centre_part), F32),
            shape((n_node, 3 * rows, LANES), F32),
            shape((1, fluid_dev), jnp.int32),
        ),
        7,
        [
            pltpu.VMEM((node_rows, LANES), jnp.int32),
            pltpu.VMEM((1, fluid_dev), jnp.int32),
            pltpu.VMEM((3, fluid_dev), F32),
            pltpu.VMEM((n_node, 3 * rows, LANES), F32),
            pltpu.VMEM((6 * fluid_dev // LANES, LANES), F32),
            dma((2, n_centre)),
            dma((2, n_node)),
            dma((2, n_node)),
            dma((2, n_node)),
            dma((3,)),
        ],
        "gather",
        0,
        [vmem(), vmem(), vmem(), smem(), anywhere, anywhere, anywhere],
    )(
        node_coords, centre_coords, disp_coef, send_count,
        send_order.reshape(node_rows, LANES), slot_perm, fluid_force,
    )
    partial, totals, places = local(
        functools.partial(pair_kernel, n_node, n_centre, rows, radius),
        (
            shape((n_centre, 6 * part_rows, LANES), F32),
            shape((n_node, 3, centre_part), F32),
            shape((1, fluid_dev), jnp.int32),
        ),
        5,
        [
            pltpu.VMEM((LANES, max(node_dev, centre_dev)), F32),
            pltpu.VMEM((node_dev, LANES), BF16),
            pltpu.VMEM((LANES, centre_dev), BF16),
            pltpu.VMEM((centre_dev, LANES), BF16),
            pltpu.VMEM((16, node_dev), F32),
            pltpu.VMEM((max(9 * node_rows, 21 * centre_dev // LANES), LANES), F32),
            pltpu.VMEM((16, centre_dev), F32),
            pltpu.VMEM((node_dev, LANES), F32),
            pltpu.VMEM((node_rows, LANES), F32),
            pltpu.VMEM((centre_dev // LANES, LANES), F32),
            pltpu.VMEM((8, node_dev), F32),
            pltpu.VMEM((8, centre_dev), F32),
            pltpu.SMEM((2, node_dev // min(512, node_dev)), jnp.int32),
        ],
        "pairs",
    )(points, centres, coeffs, got, index)
    received, centre_force = remote(
        functools.partial(reduce_kernel, n_node, n_centre, rows),
        (shape((n_node, 6 * rows, LANES), F32), shape((3, centre_part), F32)),
        3,
        [
            pltpu.VMEM((n_centre, 6 * part_rows, LANES), F32),
            pltpu.VMEM((n_node, 3, centre_part), F32),
            pltpu.VMEM((6 * part_rows, LANES), F32),
            pltpu.VMEM((n_centre, 6 * part_rows, LANES), F32),
            pltpu.VMEM((n_node, 6 * rows, LANES), F32),
            pltpu.VMEM((node_rows, LANES), F32),
            dma((2, n_centre)),
            dma((2, n_node)),
            dma((2, n_centre)),
            dma((2, n_node)),
        ],
        "reduce",
        1,
    )(partial, totals, places)
    fluid_disp = local(
        functools.partial(place_kernel, n_node, rows),
        shape((6, fluid_dev), F32),
        2,
        [pltpu.VMEM((LANES, LANES), F32)],
        "place",
    )(received, slot_perm)
    return (fluid_disp, centre_force)


def solution(mesh):
    placed = (
        P(None, ("node", "centre")),
        P(None, ("centre", "node")),
        P(None, ("centre", "node")),
        P("node", None),
        P("node", None),
        P("node", None),
        P(None, "node"),
    )
    return jax.shard_map(
        body,
        mesh=mesh,
        in_specs=placed,
        out_specs=(P(None, "node"), P(None, ("centre", "node"))),
        check_vma=False,
    )
```

```python
import functools
import math

import jax
import jax.numpy as jnp
from jax import lax
from jax.experimental import pallas as pl
from jax.experimental.pallas import tpu as pltpu
from jax.sharding import PartitionSpec as P

SUPPORT = 192
LANES = 128
F32 = jnp.float32
BF16 = jnp.bfloat16
VMEM_BYTES = 64 * 1024 * 1024 - 512 * 1024
WHOLE_VMEM = VMEM_BYTES
NT = (((1,), (1,)), ((), ()))


def vmem():
    return pl.BlockSpec(memory_space=pltpu.VMEM)


def smem():
    return pl.BlockSpec(memory_space=pltpu.SMEM)


def split(value):
    high = value.astype(BF16).astype(F32)
    return high, value - high


def onehot(index, rows):
    lanes = index.shape[1]
    return jnp.where(lax.broadcasted_iota(jnp.int32, (rows, lanes), 0) == index, 1.0, 0.0)


def scatter_part(values, index, high_rows):
    n = index.shape[1]
    low = jnp.bitwise_and(index, LANES - 1)
    high = lax.shift_right_arithmetic(index, 7)
    low_hot = onehot(low, LANES).astype(BF16)
    mask = lax.broadcasted_iota(jnp.int32, (high_rows, n), 0) == high
    stacked = jnp.concatenate(
        [jnp.where(mask, value, 0.0).astype(BF16) for value in values], axis=0
    )
    return lax.dot_general(stacked, low_hot, NT, preferred_element_type=F32)


def gather_part(lhs, index, high_rows, channels):
    n = index.shape[1]
    low = jnp.bitwise_and(index, LANES - 1)
    high = lax.shift_right_arithmetic(index, 7)
    hot = onehot(high, high_rows).astype(BF16)
    hot = jnp.concatenate([hot, hot], axis=0)
    wide = jnp.dot(lhs, hot, preferred_element_type=F32)
    mask = lax.broadcasted_iota(jnp.int32, (LANES, n), 0) == low
    rows = [
        jnp.sum(
            jnp.where(mask, wide[c * LANES : (c + 1) * LANES], 0.0), axis=0, keepdims=True
        )
        for c in range(channels)
    ]
    return jnp.concatenate(rows, axis=0)


def fill_slots(n_node, rows, perm_ref, force_ref, send_ref, acc_ref):
    fluid_dev = perm_ref.shape[1]
    high_rows = fluid_dev // LANES
    step = 1024
    for start in range(0, fluid_dev, step):
        values = []
        for c in range(3):
            values.extend(split(force_ref[c : c + 1, start : start + step]))
        part = scatter_part(values, perm_ref[:, start : start + step], high_rows)
        if start == 0:
            acc_ref[...] = part
        else:
            acc_ref[...] += part
    for c in range(3):
        base = 2 * c * high_rows
        for b in range(n_node):
            lo = base + b * rows
            send_ref[b, c * rows : (c + 1) * rows, :] = (
                acc_ref[lo : lo + rows, :]
                + acc_ref[lo + high_rows : lo + high_rows + rows, :]
            )


def find_nodes(n_node, rows, count_ref, order_ref, index_ref):
    node_rows = order_ref.shape[0]
    capacity = rows * LANES
    high, low = split(order_ref[...].astype(F32))
    lhs = jnp.transpose(
        jnp.concatenate([high, low, jnp.zeros((LANES - 2 * node_rows, LANES), F32)], axis=0)
    ).astype(BF16)[:, : 2 * node_rows]
    offset = jnp.int32(0)
    for o in range(n_node):
        count = count_ref[0, o]
        slot = lax.broadcasted_iota(jnp.int32, (1, capacity), 1)
        place = jnp.minimum(offset + slot, node_rows * LANES - 1)
        found = gather_part(lhs, place, node_rows, 1).astype(jnp.int32)
        found = jnp.where(slot < count, found, -1)
        index_ref[:, o * capacity : (o + 1) * capacity] = found
        offset = offset + count


def greet(axes):
    barrier = pltpu.get_barrier_semaphore()
    total = 0
    for name, size in axes:
        me = lax.axis_index(name)
        for d in range(1, size):
            pl.semaphore_signal(
                barrier, inc=1, device_id={name: lax.rem(me + d, size)},
                device_id_type=pl.DeviceIdType.MESH,
            )
            total += 1
    pl.semaphore_wait(barrier, total)


def spread(name, size, source, target, send_sem, recv_sem, gather):
    me = lax.axis_index(name)
    copies = []
    for d in range(1, size):
        peer = lax.rem(me + d, size)
        copy = pltpu.make_async_remote_copy(
            src_ref=source if gather else source.at[peer],
            dst_ref=target.at[me],
            send_sem=send_sem.at[d],
            recv_sem=recv_sem.at[d],
            device_id={name: peer},
            device_id_type=pl.DeviceIdType.MESH,
        )
        copy.start()
        copies.append(copy)
    return copies


def gather_kernel(
    n_node, n_centre, rows, node_ref, centre_ref, coef_ref, count_ref, order_in, perm_in, force_in,
    points_ref, centres_ref, coeffs_ref, recv_ref, index_ref,
    order_ref, perm_ref, force_ref, send_ref, acc_ref, sem_a, sem_b, sem_c, sem_d, sem_in,
):
    loads = [
        pltpu.make_async_copy(perm_in, perm_ref, sem_in.at[0]),
        pltpu.make_async_copy(force_in, force_ref, sem_in.at[1]),
        pltpu.make_async_copy(order_in, order_ref, sem_in.at[2]),
        pltpu.make_async_copy(node_ref, points_ref.at[lax.axis_index("centre")], sem_in.at[3]),
        pltpu.make_async_copy(centre_ref, centres_ref.at[lax.axis_index("node")], sem_in.at[4]),
        pltpu.make_async_copy(coef_ref, coeffs_ref.at[lax.axis_index("node")], sem_in.at[5]),
    ]
    for load in loads:
        load.start()
    greet((("node", n_node), ("centre", n_centre)))
    copies = spread("centre", n_centre, node_ref, points_ref, sem_a.at[0], sem_a.at[1], True)
    copies += spread("node", n_node, centre_ref, centres_ref, sem_b.at[0], sem_b.at[1], True)
    copies += spread("node", n_node, coef_ref, coeffs_ref, sem_c.at[0], sem_c.at[1], True)
    for load in loads:
        load.wait()
    fill_slots(n_node, rows, perm_ref, force_ref, send_ref, acc_ref)
    copies += spread("node", n_node, send_ref, recv_ref, sem_d.at[0], sem_d.at[1], False)
    me_node = lax.axis_index("node")
    recv_ref[me_node] = send_ref[me_node]
    find_nodes(n_node, rows, count_ref, order_ref, index_ref)
    for copy in copies:
        copy.wait()


def factor_rows(ref, coords, lanes, left):
    high, rest = split(coords)
    middle, low = split(rest)
    square = jnp.sum(coords * coords, axis=0, keepdims=True)
    scale = 1.0 if left else -2.0
    high, middle, low = high * scale, middle * scale, low * scale
    order = (high, high, middle, middle, high, low) if left else (high, middle, high, middle, low, high)
    for i, piece in enumerate(order):
        ref[3 * i : 3 * i + 3, lanes] = piece
    s_high, s_rest = split(square)
    s_middle, s_low = split(s_rest)
    base = 18 if left else 21
    for i, piece in enumerate((s_high, s_middle, s_low)):
        ref[base + i : base + i + 1, lanes] = piece
    base = 21 if left else 18
    ref[base : base + 3, lanes] = jnp.ones((3, square.shape[1]), F32)


BINS = 32


def table_factor(table):
    rows = table.shape[0]
    high, low = split(table)
    stacked = jnp.concatenate([high, low, jnp.zeros((LANES - 2 * rows, LANES), F32)], axis=0)
    return jnp.transpose(stacked).astype(BF16)[:, : 2 * rows]


def order_by(first, rank_ref):
    count = first.shape[1]
    bins = jnp.minimum((first * BINS).astype(jnp.int32), BINS - 1)
    member = onehot(bins, BINS)
    below = jnp.where(lax.broadcasted_iota(jnp.int32, (BINS, count), 0) > bins, 1.0, 0.0)
    carry = jnp.sum(below, axis=1, keepdims=True)
    chunks = count // LANES
    stacked = jnp.concatenate(
        [member[:, k * LANES : (k + 1) * LANES] for k in range(chunks)], axis=0
    )
    upper = jnp.where(
        lax.broadcasted_iota(jnp.int32, (LANES, LANES), 0)
        <= lax.broadcasted_iota(jnp.int32, (LANES, LANES), 1),
        1.0,
        0.0,
    ).astype(BF16)
    running = jnp.dot(stacked.astype(BF16), upper, preferred_element_type=F32)
    for k in range(chunks):
        part = running[k * BINS : (k + 1) * BINS]
        mine = stacked[k * BINS : (k + 1) * BINS]
        rank_ref[k : k + 1, :] = jnp.sum(mine * (part + carry), axis=0, keepdims=True) - 1.0
        carry = carry + part[:, LANES - 1 : LANES]


def rank_row(rank_ref, first, last):
    return jnp.concatenate([rank_ref[k : k + 1, :] for k in range(first, last)], axis=1).astype(
        jnp.int32
    )


def pair_kernel(
    n_node, n_centre, rows, radius, points_ref, centres_ref, coeffs_ref, recv_ref, index_ref,
    disp_ref, total_ref, place_ref,
    wide_ref, left_ref, right_ref, coef_ref, force_ref, acc_ref, facc_ref, dacc_ref,
    node_rank, centre_rank, node_sorted, centre_sorted, limit_ref,
):
    node_part = points_ref.shape[2]
    node_dev = node_part * n_centre
    centre_part = centres_ref.shape[2]
    centre_dev = centre_part * n_node
    node_rows, centre_rows = node_dev // LANES, centre_dev // LANES
    capacity = rows * LANES
    inverse = 1.0 / radius
    tile_g, tile_j = min(512, node_dev), min(512, centre_dev)
    n_g, n_j = node_dev // tile_g, centre_dev // tile_j
    order_by(jnp.concatenate([points_ref[z][0:1, :] for z in range(n_centre)], axis=1), node_rank)
    order_by(jnp.concatenate([centres_ref[o][0:1, :] for o in range(n_node)], axis=1), centre_rank)

    def thirds(value):
        high, rest = split(value)
        middle, low = split(rest)
        return [piece[c : c + 1] for piece in (high, middle, low) for c in range(3)]

    used = 9 * node_rows
    for z in range(n_centre):
        per = node_part // LANES
        place = rank_row(node_rank, z * per, (z + 1) * per)
        part = scatter_part(thirds(points_ref[z]), place, node_rows)
        acc_ref[0:used, :] = part if z == 0 else acc_ref[0:used, :] + part
    for h in range(node_rows):
        piece = [acc_ref[pl.ds(3 * i * node_rows + h, 3, stride=node_rows), :] for i in range(3)]
        node_sorted[0:3, h * LANES : (h + 1) * LANES] = piece[0] + piece[1] + piece[2]
    used = 21 * centre_rows
    for o in range(n_node):
        per = centre_part // LANES
        place = rank_row(centre_rank, o * per, (o + 1) * per)
        high, low = split(coeffs_ref[o] * 4.0)
        values = thirds(centres_ref[o]) + [p[c : c + 1] for p in (high, low) for c in range(6)]
        part = scatter_part(values, place, centre_rows)
        acc_ref[0:used, :] = part if o == 0 else acc_ref[0:used, :] + part
    wide_ref[...] = jnp.zeros_like(wide_ref)
    for h in range(centre_rows):
        lanes = slice(h * LANES, (h + 1) * LANES)
        piece = [
            acc_ref[pl.ds(3 * i * centre_rows + h, 3, stride=centre_rows), :] for i in range(3)
        ]
        centre_sorted[0:3, lanes] = piece[0] + piece[1] + piece[2]
        wide_ref[0:6, lanes] = acc_ref[pl.ds(9 * centre_rows + h, 6, stride=centre_rows), :]
        wide_ref[8:14, lanes] = acc_ref[pl.ds(15 * centre_rows + h, 6, stride=centre_rows), :]
    for start in range(0, centre_dev, 512):
        coef_ref[start : start + 512, :] = jnp.transpose(wide_ref[:, start : start + 512]).astype(BF16)
    factor = table_factor(node_rank[...])
    used = 6 * node_rows
    for o in range(n_node):
        slots = slice(o * capacity, (o + 1) * capacity)
        index = index_ref[:, slots]
        place = gather_part(factor, index, node_rows, 1).astype(jnp.int32)
        place = jnp.where(index < 0, -1, place)
        place_ref[:, slots] = place
        values = []
        for c in range(3):
            row = jnp.concatenate(
                [recv_ref[o, c * rows + r : c * rows + r + 1, :] for r in range(rows)], axis=1
            )
            values.append(split(row))
        values = [v[0] for v in values] + [v[1] for v in values]
        part = scatter_part(values, place, node_rows)
        acc_ref[0:used, :] = part if o == 0 else acc_ref[0:used, :] + part
    force_ref[...] = jnp.zeros_like(force_ref)
    for h in range(node_rows):
        lanes = slice(h * LANES, (h + 1) * LANES)
        force_ref[0:6, lanes] = acc_ref[pl.ds(h, 6, stride=node_rows), :] * 4.0
    wide_ref[...] = jnp.zeros_like(wide_ref)
    for start in range(0, node_dev, 1024):
        lanes = slice(start, start + 1024)
        factor_rows(wide_ref, (node_sorted[0:3, lanes] - 0.5) * inverse, lanes, True)
    for start in range(0, node_dev, 512):
        left_ref[start : start + 512, :] = jnp.transpose(wide_ref[:, start : start + 512]).astype(BF16)
    wide_ref[...] = jnp.zeros_like(wide_ref)
    for start in range(0, centre_dev, 512):
        lanes = slice(start, start + 512)
        factor_rows(wide_ref, (centre_sorted[0:3, lanes] - 0.5) * inverse, lanes, False)
    right_ref[...] = wide_ref[...].astype(BF16)
    reach = radius * 1.00001
    upto, since = [], []
    for j in range(n_j):
        row = centre_sorted[0:1, j * tile_j : (j + 1) * tile_j]
        upto.append(jnp.max(row))
        since.append(jnp.min(row))
    for j in range(1, n_j):
        upto[j] = jnp.maximum(upto[j], upto[j - 1])
    for j in range(n_j - 2, -1, -1):
        since[j] = jnp.minimum(since[j], since[j + 1])
    for i in range(n_g):
        row = node_sorted[0:1, i * tile_g : (i + 1) * tile_g]
        least, most = jnp.min(row) - reach, jnp.max(row) + reach
        before, after = jnp.int32(0), jnp.int32(n_j)
        for j in range(n_j):
            before = before + jnp.where(upto[j] < least, 1, 0)
            after = after - jnp.where(since[j] > most, 1, 0)
        limit_ref[0, i] = before
        limit_ref[1, i] = after
    facc_ref[...] = jnp.zeros_like(facc_ref)
    dacc_ref[...] = jnp.zeros_like(dacc_ref)

    @pl.loop(0, n_g)
    def _(i):
        at = pl.ds(pl.multiple_of(i * tile_g, tile_g), tile_g)

        @pl.loop(limit_ref[0, i], limit_ref[1, i])
        def _(j):
            columns = pl.ds(pl.multiple_of(j * tile_j, tile_j), tile_j)
            force = force_ref[:, at].astype(BF16)
            squared = jnp.dot(left_ref[at, :], right_ref[:, columns], preferred_element_type=F32)
            squared = jnp.maximum(squared, 1e-20)
            scaled = squared * lax.rsqrt(squared)
            remain = jnp.maximum(1.0 - scaled, 0.0)
            remain = remain * remain
            remain = remain * remain
            basis = remain * (scaled + 0.25)
            high = basis.astype(BF16)
            low = (basis - high.astype(F32)).astype(BF16)
            weights = coef_ref[columns, :]
            dacc_ref[at, :] += jnp.dot(high, weights, preferred_element_type=F32) + jnp.dot(
                low, weights, preferred_element_type=F32
            )
            facc_ref[:, columns] += jnp.dot(force, high, preferred_element_type=F32) + jnp.dot(
                force, low, preferred_element_type=F32
            )

    part_rows = node_part // LANES
    for z in range(n_centre):
        for r in range(part_rows):
            start = z * node_part + r * LANES
            turned = jnp.transpose(dacc_ref[start : start + LANES, :])
            disp_ref[z, pl.ds(r, 6, stride=part_rows), :] = turned[0:6] + turned[8:14]
    for h in range(centre_rows):
        lanes = slice(h * LANES, (h + 1) * LANES)
        acc_ref[pl.ds(h, 3, stride=centre_rows), :] = facc_ref[0:3, lanes] + facc_ref[3:6, lanes]
    factor = jnp.concatenate(
        [table_factor(acc_ref[c * centre_rows : (c + 1) * centre_rows, :]) for c in range(3)],
        axis=0,
    )
    for o in range(n_node):
        per = centre_part // LANES
        place = rank_row(centre_rank, o * per, (o + 1) * per)
        total_ref[o] = gather_part(factor, place, centre_rows, 3)


def reduce_kernel(
    n_node, n_centre, rows, disp_ref, total_ref, index_ref, recv_ref, force_ref,
    got_disp, got_force, mine_ref, whole_ref, send_ref, tab_ref, sem_a, sem_b, sem_c, sem_d,
):
    greet((("node", n_node), ("centre", n_centre)))
    me_node, me_centre = lax.axis_index("node"), lax.axis_index("centre")
    copies = spread("centre", n_centre, disp_ref, got_disp, sem_a.at[0], sem_a.at[1], False)
    later = spread("node", n_node, total_ref, got_force, sem_b.at[0], sem_b.at[1], False)
    got_disp[me_centre] = disp_ref[me_centre]
    got_force[me_node] = total_ref[me_node]
    for copy in copies:
        copy.wait()
    total = got_disp[0]
    for z in range(1, n_centre):
        total = total + got_disp[z]
    mine_ref[...] = total
    whole_ref[me_centre] = total
    copies = spread("centre", n_centre, mine_ref, whole_ref, sem_c.at[0], sem_c.at[1], True)
    for copy in later:
        copy.wait()
    total = got_force[0]
    for o in range(1, n_node):
        total = total + got_force[o]
    force_ref[...] = total
    for copy in copies:
        copy.wait()
    part_rows = whole_ref.shape[1] // 6
    node_rows = part_rows * n_centre
    capacity = rows * LANES
    factor = []
    for c in range(6):
        for z in range(n_centre):
            tab_ref[z * part_rows : (z + 1) * part_rows, :] = whole_ref[
                z, c * part_rows : (c + 1) * part_rows, :
            ]
        factor.append(table_factor(tab_ref[...]))
    factor = jnp.concatenate(factor, axis=0)
    copies = []
    for d in list(range(1, n_node)) + [0]:
        peer = lax.rem(me_node + d, n_node)
        slots = pl.ds(pl.multiple_of(peer * capacity, LANES), capacity)
        got = gather_part(factor, index_ref[:, slots], node_rows, 6)
        for r in range(rows):
            send_ref[d, pl.ds(r, 6, stride=rows), :] = got[:, r * LANES : (r + 1) * LANES]
        if d == 0:
            continue
        copy = pltpu.make_async_remote_copy(
            src_ref=send_ref.at[d],
            dst_ref=recv_ref.at[me_node],
            send_sem=sem_d.at[0, d],
            recv_sem=sem_d.at[1, d],
            device_id={"node": peer},
            device_id_type=pl.DeviceIdType.MESH,
        )
        copy.start()
        copies.append(copy)
    recv_ref[me_node] = send_ref[0]
    for copy in copies:
        copy.wait()


def place_kernel(n_node, rows, recv_ref, perm_ref, out_ref, tab_ref):
    high_rows = n_node * rows
    lhs = []
    for c in range(6):
        for o in range(n_node):
            high, low = split(recv_ref[o, c * rows : (c + 1) * rows, :])
            tab_ref[o * rows : (o + 1) * rows, :] = high
            tab_ref[high_rows + o * rows : high_rows + (o + 1) * rows, :] = low
        lhs.append(jnp.transpose(tab_ref[...]).astype(BF16))
    lhs = jnp.concatenate(lhs, axis=0)
    fluid_dev = perm_ref.shape[1]
    step = 1024
    for start in range(0, fluid_dev, step):
        out_ref[:, start : start + step] = gather_part(
            lhs, perm_ref[:, start : start + step], high_rows, 6
        )


def body(node_coords, centre_coords, disp_coef, send_count, send_order, slot_perm, fluid_force):
    n_node = lax.axis_size("node")
    n_centre = lax.axis_size("centre")
    node_dev = send_order.shape[1]
    fluid_dev = slot_perm.shape[1]
    capacity = fluid_dev // n_node
    rows = capacity // LANES
    node_rows = node_dev // LANES
    centre_part = centre_coords.shape[1]
    centre_total = centre_part * n_node * n_centre
    centre_dev = centre_part * n_node
    node_part = node_coords.shape[1]
    part_rows = node_part // LANES
    radius = (0.75 * SUPPORT / (math.pi * centre_total)) ** (1.0 / 3.0)
    dma = pltpu.SemaphoreType.DMA
    shape = jax.ShapeDtypeStruct

    def local(function, outs, n_in, scratch, name, specs=None):
        return pl.pallas_call(
            function,
            out_shape=outs,
            in_specs=specs or [vmem()] * n_in,
            out_specs=jax.tree.map(lambda _: vmem(), outs),
            scratch_shapes=scratch,
            name=name,
            compiler_params=pltpu.CompilerParams(vmem_limit_bytes=VMEM_BYTES),
        )

    def remote(function, outs, n_in, scratch, name, number, specs=None, limit=VMEM_BYTES):
        return pl.pallas_call(
            function,
            out_shape=outs,
            in_specs=specs or [vmem()] * n_in,
            out_specs=jax.tree.map(lambda _: vmem(), outs),
            scratch_shapes=scratch,
            name=name,
            compiler_params=pltpu.CompilerParams(
                vmem_limit_bytes=limit, collective_id=number, has_side_effects=True
            ),
        )

    far = pl.BlockSpec(memory_space=pltpu.HBM)
    points, centres, coeffs, got, index = remote(
        functools.partial(gather_kernel, n_node, n_centre, rows),
        (
            shape((n_centre, 3, node_part), F32),
            shape((n_node, 3, centre_part), F32),
            shape((n_node, 6, centre_part), F32),
            shape((n_node, 3 * rows, LANES), F32),
            shape((1, fluid_dev), jnp.int32),
        ),
        7,
        [
            pltpu.VMEM((node_rows, LANES), jnp.int32),
            pltpu.VMEM((1, fluid_dev), jnp.int32),
            pltpu.VMEM((3, fluid_dev), F32),
            pltpu.VMEM((n_node, 3 * rows, LANES), F32),
            pltpu.VMEM((6 * fluid_dev // LANES, LANES), F32),
            dma((2, n_centre)),
            dma((2, n_node)),
            dma((2, n_node)),
            dma((2, n_node)),
            dma((6,)),
        ],
        "gather",
        0,
        [far, far, far, smem(), far, far, far],
        WHOLE_VMEM,
    )(
        node_coords, centre_coords, disp_coef, send_count,
        send_order.reshape(node_rows, LANES), slot_perm, fluid_force,
    )
    partial, totals, places = local(
        functools.partial(pair_kernel, n_node, n_centre, rows, radius),
        (
            shape((n_centre, 6 * part_rows, LANES), F32),
            shape((n_node, 3, centre_part), F32),
            shape((1, fluid_dev), jnp.int32),
        ),
        5,
        [
            pltpu.VMEM((LANES, max(node_dev, centre_dev)), F32),
            pltpu.VMEM((node_dev, LANES), BF16),
            pltpu.VMEM((LANES, centre_dev), BF16),
            pltpu.VMEM((centre_dev, LANES), BF16),
            pltpu.VMEM((16, node_dev), F32),
            pltpu.VMEM((max(9 * node_rows, 21 * centre_dev // LANES), LANES), F32),
            pltpu.VMEM((16, centre_dev), F32),
            pltpu.VMEM((node_dev, LANES), F32),
            pltpu.VMEM((node_rows, LANES), F32),
            pltpu.VMEM((centre_dev // LANES, LANES), F32),
            pltpu.VMEM((8, node_dev), F32),
            pltpu.VMEM((8, centre_dev), F32),
            pltpu.SMEM((2, node_dev // min(512, node_dev)), jnp.int32),
        ],
        "pairs",
    )(points, centres, coeffs, got, index)
    received, centre_force = remote(
        functools.partial(reduce_kernel, n_node, n_centre, rows),
        (shape((n_node, 6 * rows, LANES), F32), shape((3, centre_part), F32)),
        3,
        [
            pltpu.VMEM((n_centre, 6 * part_rows, LANES), F32),
            pltpu.VMEM((n_node, 3, centre_part), F32),
            pltpu.VMEM((6 * part_rows, LANES), F32),
            pltpu.VMEM((n_centre, 6 * part_rows, LANES), F32),
            pltpu.VMEM((n_node, 6 * rows, LANES), F32),
            pltpu.VMEM((node_rows, LANES), F32),
            dma((2, n_centre)),
            dma((2, n_node)),
            dma((2, n_centre)),
            dma((2, n_node)),
        ],
        "reduce",
        1,
    )(partial, totals, places)
    fluid_disp = local(
        functools.partial(place_kernel, n_node, rows),
        shape((6, fluid_dev), F32),
        2,
        [pltpu.VMEM((LANES, LANES), F32)],
        "place",
    )(received, slot_perm)
    return (fluid_disp, centre_force)


def solution(mesh):
    placed = (
        P(None, ("node", "centre")),
        P(None, ("centre", "node")),
        P(None, ("centre", "node")),
        P("node", None),
        P("node", None),
        P("node", None),
        P(None, "node"),
    )
    return jax.shard_map(
        body,
        mesh=mesh,
        in_specs=placed,
        out_specs=(P(None, "node"), P(None, ("centre", "node"))),
        check_vma=False,
    )
```
